128 devices in a mesh: seq: 16 (over y, x_hi, core), col: 8 (over z, x_lo).
Axes of the slice: x: 4 (x_hi: 2, x_lo: 2; x = x_hi * 2 + x_lo), y: 4, z: 4, core: 2. Of those that a mesh axis runs over, the one named last changes fastest.
Arguments:
- features: bfloat16 [64, 64, 512], P('seq', 'col'), may hold values from -6 to 6
- conv_weight: bfloat16 [3, 3, 512, 512], replicated, may hold values from -0.09375 to 0.09375
- w_query_key: bfloat16 [512, 2, 4096], P(None, None, 'col'), may hold values from -0.375 to 0.375
- w_value: bfloat16 [512, 4096], P(None, 'col'), may hold values from -1 to 1
- text_qkv: bfloat16 [1024, 3, 4096], P('seq', None, 'col')
- span_ids: int32 [5120], replicated, may hold values from -1 to 15, as said below
- out_cot: bfloat16 [5120, 4096], P('seq', 'col'), may hold values from -6 to 6
Outputs:
- attended: bfloat16 [5120, 4096], P('seq', 'col')
- feature_grad: bfloat16 [64, 64, 512], P('seq', 'col')
- text_grad: bfloat16 [1024, 3, 4096], P('seq', None, 'col')
The draws below stay inside these ranges and needn't reach their ends.
Inputs may be any that keep to these rules, and one draw needn't show every extreme that they name: `span_ids`: the positions form aligned blocks of 320, one for each index of seq. In each block exactly 256 positions carry an id of 0 or more, in one run without gaps; all others are text. An image span is the run of one block, or the runs of two consecutive blocks where the first run ends its block and the second begins its block; its id is the index of its first block.
All inputs are finite; a program needn't handle non-finite values.
Results may differ from the reference program's by a relative error of at most 0.034.
The reference program's roundings to bfloat16 on the way (of `act`, `encoded`, `image_qkv`, `mixed`, `weights`, `score_grad`, `mixed_grad` and `encoded_grad`) count: a program that leaves them out, or rounds other values in their place, can miss the bound.
Values may be sent and summed in bfloat16 or wider, within the bound.
No kernel may reach another device: no remote copies, remote signals or barrier semaphores. Data moves between devices by JAX's collectives and lax.ppermute only.
A program may use at most 128 MiB of HBM per device.

```python
import math
import jax
import jax.numpy as jnp
from jax import lax

HEADS = 32
HD = 128
C = 512
TXT_DEV = 64
D = 4096
H = 64
W = 64
IMG_DEV = 256
TOK_DEV = 320
TOKENS = 5120
TXT_TOKENS = 1024


def draw_span_ids(key, part):
    key = jax.random.fold_in(key, 11)
    pair_key, start_key = jax.random.split(key)
    blocks = TOKENS // TOK_DEV
    block_index = jnp.arange(blocks, dtype=jnp.int32)
    pair_bits = jax.random.randint(pair_key, (blocks,), 0, 2)
    joins_next = (block_index % 2 == 0) & (block_index + 2 < blocks) & (pair_bits == 1)
    joins_prev = jnp.concatenate([jnp.zeros((1,), jnp.bool_), joins_next[:-1]])
    free_start = jax.random.randint(start_key, (blocks,), 0, TXT_DEV + 1)
    run_start = jnp.where(joins_next, TXT_DEV, jnp.where(joins_prev, 0, free_start))
    span_of_block = jnp.where(joins_prev, block_index - 1, block_index)
    offsets = jnp.arange(TOK_DEV, dtype=jnp.int32)
    inside = (offsets[None, :] >= run_start[:, None]) & (offsets[None, :] < run_start[:, None] + IMG_DEV)
    return jnp.where(inside, span_of_block[:, None], -1).reshape(TOKENS).astype(jnp.int32)


def draw_text_qkv(key, part):
    key = jax.random.fold_in(key, 5)
    base_key = jax.random.fold_in(key, 0)
    shape = (TXT_TOKENS, 3, D)
    factors = jnp.array([1.7, 1.7, 4.0], jnp.float32)[None, :, None]
    drawn = jax.random.normal(base_key, shape, jnp.float32) * factors
    return drawn.astype(jnp.bfloat16)


def block_levels(own_key, shape, cuts, least, high):
    loudness, own = 1.0, jax.random.fold_in(own_key, 6)
    for position, parts in cuts:
        steps = jnp.exp(jax.random.uniform(jax.random.fold_in(own, position), (parts,), jnp.float32, least / len(cuts), high / len(cuts)))
        loudness = loudness * jnp.repeat(steps, shape[position] // parts).reshape([-1 if axis == position else 1 for axis in range(len(shape))])
    return loudness


def bell_draw(key, dims, spread, limit, pieces=(), held_as=jnp.bfloat16):
    values = spread * jax.random.normal(key, dims, jnp.float32)
    if pieces:
        values = values * block_levels(key, dims, pieces, -0.22, 0.18)
    return jnp.clip(values, -limit, limit).astype(held_as)


def setup_inputs(seed: int = 0) -> dict:
    key_of = jax.random.split(jax.random.key(seed), 8)
    return {
        "features": bell_draw(key_of[0], (H, W, C), 1.0, 6.0, ((0, 16), (1, 8))),
        "conv_weight": bell_draw(key_of[1], (3, 3, C, C), (9 * C) ** -0.5, 0.09375),
        "w_query_key": bell_draw(key_of[2], (C, 2, D), (C // 2) ** -0.5, 0.375, ((2, 8),)),
        "w_value": bell_draw(key_of[3], (C, D), (C // 16) ** -0.5, 1.0, ((1, 8),)),
        "text_qkv": draw_text_qkv(jax.random.fold_in(key_of[7], 71), 0),
        "span_ids": draw_span_ids(jax.random.fold_in(key_of[7], 71), 0),
        "out_cot": bell_draw(key_of[6], (TOKENS, D), 1.0, 6.0, ((0, 16), (1, 8))),
    }


def silu_slope(value):
    sigma = jax.nn.sigmoid(value)
    return sigma * (1.0 + value * (1.0 - sigma))

def conv_apply(padded, weight, transposed):
    height = padded.shape[0] - 2
    width = padded.shape[1] - 2
    channels = padded.shape[2]
    out_channels = weight.shape[2] if transposed else weight.shape[3]
    running = jnp.zeros((height * width, out_channels), jnp.float32)
    for a in range(3):
        for b in range(3):
            window = padded[a:a + height, b:b + width, :].reshape(height * width, channels)
            if transposed:
                running = running + lax.dot_general(window, weight[2 - a, 2 - b], (((1,), (1,)), ((), ())), preferred_element_type=jnp.float32)
            else:
                running = running + jnp.dot(window, weight[a, b], preferred_element_type=jnp.float32)
    return running.reshape(height, width, out_channels)

def reference(features, conv_weight, w_query_key, w_value, text_qkv, span_ids, out_cot):
    inv_root = 1.0 / math.sqrt(HD)
    feature_wide = features.astype(jnp.float32)
    act = jax.nn.silu(feature_wide).astype(jnp.bfloat16)
    act_padded = jnp.pad(act, ((1, 1), (1, 1), (0, 0)))
    encoded = (feature_wide + conv_apply(act_padded, conv_weight, False)).astype(jnp.bfloat16)
    w_joined = jnp.concatenate([w_query_key.reshape(C, 2 * D), w_value], axis=1)
    image_qkv = jnp.dot(encoded.reshape(H * W, C), w_joined, preferred_element_type=jnp.float32).astype(jnp.bfloat16)
    text_flat = text_qkv.reshape(TXT_TOKENS, 3 * D)
    is_image = span_ids >= 0
    image_flag = is_image.astype(jnp.int32)
    image_rank = jnp.maximum(jnp.cumsum(image_flag) - 1, 0).astype(jnp.int32)
    text_rank = jnp.maximum(jnp.cumsum(1 - image_flag) - 1, 0).astype(jnp.int32)
    mixed = jnp.where(is_image[:, None], jnp.take(image_qkv, image_rank, axis=0), jnp.take(text_flat, text_rank, axis=0))
    positions = jnp.arange(TOKENS, dtype=jnp.int32)
    visible = (positions[None, :] <= positions[:, None]) | (span_ids[:, None] >= 0) & (span_ids[:, None] == span_ids[None, :])

    def by_head(flat):
        return jnp.transpose(flat.reshape(TOKENS, HEADS, HD), (1, 0, 2))

    def by_token(stacked):
        return jnp.transpose(stacked, (1, 0, 2)).reshape(TOKENS, D)

    def per_head(operands):
        head_query, head_key, head_value, head_cot = operands
        scores = jnp.dot(head_query, head_key.T, preferred_element_type=jnp.float32) * inv_root
        log_total = jax.nn.logsumexp(jnp.where(visible, scores, -jnp.inf), axis=1)
        probs = jnp.exp(jnp.where(visible, scores - log_total[:, None], -jnp.inf))
        weights = probs.astype(jnp.bfloat16)
        attended = jnp.dot(weights, head_value, preferred_element_type=jnp.float32).astype(jnp.bfloat16)
        delta = lax.optimization_barrier(jnp.sum(head_cot.astype(jnp.float32) * attended.astype(jnp.float32), axis=1))
        prob_grad = jnp.dot(head_cot, head_value.T, preferred_element_type=jnp.float32)
        score_grad = (probs * (prob_grad - delta[:, None]) * inv_root).astype(jnp.bfloat16)
        query_grad = jnp.dot(score_grad, head_key, preferred_element_type=jnp.float32).astype(jnp.bfloat16)
        key_grad = jnp.dot(score_grad.T, head_query, preferred_element_type=jnp.float32).astype(jnp.bfloat16)
        value_grad = jnp.dot(weights.T, head_cot, preferred_element_type=jnp.float32).astype(jnp.bfloat16)
        return (attended, query_grad, key_grad, value_grad)
    outputs = lax.map(per_head, (by_head(mixed[:, :D]), by_head(mixed[:, D:2 * D]), by_head(mixed[:, 2 * D:]), by_head(out_cot)))
    attended = by_token(outputs[0])
    mixed_grad = jnp.concatenate([by_token(outputs[1]), by_token(outputs[2]), by_token(outputs[3])], axis=1)
    order = jnp.argsort(image_flag, stable=True).astype(jnp.int32)
    text_grad = jnp.take(mixed_grad, order[:TXT_TOKENS], axis=0).reshape(TXT_TOKENS, 3, D)
    image_grad = jnp.take(mixed_grad, order[TXT_TOKENS:], axis=0)
    encoded_grad = jnp.dot(image_grad, w_joined.T, preferred_element_type=jnp.float32).astype(jnp.bfloat16).reshape(H, W, C)
    act_grad = conv_apply(jnp.pad(encoded_grad, ((1, 1), (1, 1), (0, 0))), conv_weight, True)
    feature_grad = (encoded_grad.astype(jnp.float32) + silu_slope(feature_wide) * act_grad).astype(jnp.bfloat16)
    return (attended, feature_grad, text_grad)
```

```python
import math

import jax
import jax.numpy as jnp
from jax import lax
from jax.experimental import pallas as pl
from jax.experimental.pallas import tpu as pltpu
from jax.sharding import PartitionSpec as P

HD = 128
TXT = 64
IMG = 256
TOK = 320
GRP = 4 * TOK
TILE = 256
NT = GRP // TILE
SCALE = HD ** -0.5
SCALE2 = SCALE * math.log2(math.e)
NEG = -1e30
BF = jnp.bfloat16
F32 = jnp.float32
VLIM = 56 * 1024 * 1024


def dot_nt(a, b):
    return lax.dot_general(a, b, (((1,), (1,)), ((), ())), preferred_element_type=F32)


def dot_nn(a, b):
    return lax.dot_general(a, b, (((1,), (0,)), ((), ())), preferred_element_type=F32)


def vmem():
    return pl.BlockSpec(memory_space=pltpu.VMEM)


def smem():
    return pl.BlockSpec(memory_space=pltpu.SMEM)


def encode_kernel(y_ref, band_ref, conv_ref, w_ref, text_ref, *rest):
    kv_refs, q_refs = rest[:4], rest[4:8]
    act_ref, acc_ref = rest[8:]
    rows = band_ref.shape[0]
    cells = rows - 2 * 64
    y = y_ref[0]
    wide = band_ref[...].astype(F32)
    act = (wide / (1.0 + jnp.exp(-wide))).astype(BF).astype(F32)
    column = lax.broadcasted_iota(jnp.int32, act.shape, 0) % 64
    act_ref[0] = jnp.where(column == 0, 0.0, pltpu.roll(act, 1, 0)).astype(BF)
    act_ref[1] = act.astype(BF)
    act_ref[2] = jnp.where(column == 63, 0.0, pltpu.roll(act, rows - 1, 0)).astype(BF)
    acc_ref[...] = band_ref[64 : 64 + cells, :].astype(F32)
    for a in range(3):
        for b in range(3):
            acc_ref[...] += dot_nn(act_ref[b, a * 64 : a * 64 + cells, :], conv_ref[a, b])
    encoded = acc_ref[...].astype(BF)
    for s in range(4):
        head = lax.rem(y + s, 4)
        qkv = dot_nn(encoded, w_ref[head]).astype(BF)
        text = text_ref[head]
        q_refs[s][:TXT, :] = text[:, :HD]
        q_refs[s][TXT:, :] = qkv[:, :HD]
        kv_refs[s][:TXT, :] = text[:, HD:]
        kv_refs[s][TXT:, :] = qkv[:, HD:]


def encode(y, band, conv_weight, w_heads, text_heads):
    return pl.pallas_call(
        encode_kernel,
        out_shape=[jax.ShapeDtypeStruct((TOK, 2 * HD), BF)] * 4 + [jax.ShapeDtypeStruct((TOK, HD), BF)] * 4,
        in_specs=[smem()] + [vmem()] * 4,
        out_specs=[vmem()] * 8,
        scratch_shapes=[pltpu.VMEM((3,) + band.shape, BF), pltpu.VMEM((band.shape[0] - 128, band.shape[1]), F32)],
        compiler_params=pltpu.CompilerParams(vmem_limit_bytes=VLIM),
        name="encode",
    )(y, band, conv_weight, w_heads, text_heads)


def attention_kernel(meta_ref, qpos_ref, qspan_ref, kpos_ref, kspan_ref, *rest):
    q_in, g_in, kv_in = rest[0:4], rest[4:8], rest[8:24]
    att_out, dq_out, dkv_out = rest[24:28], rest[28:32], rest[32:48]
    q_ref, qt_ref, g_ref, gt_ref, k_ref, v_ref, s_ref, dk_ref, dv_ref, m_ref, l_ref, o_ref, d_ref = rest[48:]
    y = meta_ref[0]
    for s in range(4):
        slot = lax.rem(y + 4 - s, 4)
        q_ref[slot] = q_in[s][...]
        qt_ref[slot] = q_in[s][...].T
        g_ref[slot] = g_in[s][...]
        gt_ref[slot] = g_in[s][...].T
        for rel in range(4):
            k_ref[slot, rel * TOK : (rel + 1) * TOK, :] = kv_in[4 * rel + s][:, :HD]
            v_ref[slot, rel * TOK : (rel + 1) * TOK, :] = kv_in[4 * rel + s][:, HD:]
    dk_ref[...] = jnp.zeros_like(dk_ref)
    dv_ref[...] = jnp.zeros_like(dv_ref)

    def fold(x, op):
        return op(x[:, :HD], x[:, HD:])

    def query_slot(slot, unused):
        queries, grads = q_ref[slot], g_ref[slot]
        queries_t, grads_t = qt_ref[slot], gt_ref[slot]
        join = meta_ref[1 + slot]
        m_ref[...] = jnp.full_like(m_ref, NEG)
        l_ref[...] = jnp.zeros_like(l_ref)
        o_ref[...] = jnp.zeros_like(o_ref)

        def every(step):
            def full(group, unused):
                for t in range(NT):
                    step(group, t, False)
                return unused

            lax.fori_loop(0, slot, full, 0)
            for t in range(NT):
                step(slot, t, True)

            @pl.when(join > 0)
            def _():
                for t in range(NT - 2, NT):
                    step(slot + 1, t, True)

        def score_step(group, t, masked):
            cols = slice(t * TILE, (t + 1) * TILE)
            scores = dot_nt(queries, k_ref[group, cols, :])
            if masked:
                seen = (kpos_ref[group, :, cols] <= qpos_ref[slot]) | (kspan_ref[group, :, cols] == qspan_ref[slot])
                scores = jnp.where(seen, scores, NEG)
            s_ref[group, :, cols] = scores
            m_ref[...] = jnp.maximum(m_ref[...], fold(scores, jnp.maximum))

        every(score_step)
        peak = jnp.broadcast_to(jnp.max(m_ref[...], axis=1, keepdims=True) * SCALE2, (TOK, TILE))

        def weight_step(group, t, masked):
            cols = slice(t * TILE, (t + 1) * TILE)
            weights = jnp.exp2(s_ref[group, :, cols] * SCALE2 - peak)
            s_ref[group, :, cols] = weights
            l_ref[...] += fold(weights, jnp.add)
            o_ref[...] += dot_nn(weights.astype(BF), v_ref[group, cols, :])

        every(weight_step)
        inverse = 1.0 / jnp.sum(l_ref[...], axis=1, keepdims=True)
        attended = (o_ref[...] * inverse).astype(BF)
        m_ref[...] = attended.astype(F32)
        delta = jnp.broadcast_to(
            jnp.sum(grads.astype(F32) * attended.astype(F32), axis=1, keepdims=True), (TOK, TILE)
        )
        inverse = jnp.broadcast_to(inverse, (TOK, TILE))
        d_ref[...] = jnp.zeros_like(d_ref)

        def grad_step(group, t, masked):
            cols = slice(t * TILE, (t + 1) * TILE)
            probs = s_ref[group, :, cols] * inverse
            prob_grad = dot_nt(grads, v_ref[group, cols, :])
            score_grad = (probs * (prob_grad - delta)).astype(BF)
            d_ref[...] += dot_nn(score_grad, k_ref[group, cols, :])
            dk_ref[group, :, cols] += dot_nn(queries_t, score_grad)
            dv_ref[group, :, cols] += dot_nn(grads_t, probs.astype(BF))

        every(grad_step)
        s = lax.rem(y + 4 - slot, 4)
        for t in range(4):

            @pl.when(s == t)
            def _(t=t):
                att_out[t][...] = m_ref[...].astype(BF)
                dq_out[t][...] = (d_ref[...] * SCALE).astype(BF)

        return unused

    lax.fori_loop(0, 4, query_slot, 0)
    for s in range(4):
        slot = lax.rem(y + 4 - s, 4)
        key_grad = (dk_ref[slot] * SCALE).T.astype(BF)
        value_grad = dv_ref[slot].T.astype(BF)
        for rel in range(4):
            dkv_out[4 * rel + s][:, :HD] = key_grad[rel * TOK : (rel + 1) * TOK]
            dkv_out[4 * rel + s][:, HD:] = value_grad[rel * TOK : (rel + 1) * TOK]


def attention(meta, qpos, qspan, kpos, kspan, q, g, kv):
    narrow, double = jax.ShapeDtypeStruct((TOK, HD), BF), jax.ShapeDtypeStruct((TOK, 2 * HD), BF)
    out = pl.pallas_call(
        attention_kernel,
        out_shape=[narrow] * 8 + [double] * 16,
        in_specs=[smem()] + [vmem()] * 28,
        out_specs=[vmem()] * 24,
        scratch_shapes=[
            pltpu.VMEM((4, TOK, HD), BF),
            pltpu.VMEM((4, HD, TOK), BF),
            pltpu.VMEM((4, TOK, HD), BF),
            pltpu.VMEM((4, HD, TOK), BF),
            pltpu.VMEM((4, GRP, HD), BF),
            pltpu.VMEM((4, GRP, HD), BF),
            pltpu.VMEM((4, TOK, GRP), F32),
            pltpu.VMEM((4, HD, GRP), F32),
            pltpu.VMEM((4, HD, GRP), F32),
            pltpu.VMEM((TOK, HD), F32),
            pltpu.VMEM((TOK, HD), F32),
            pltpu.VMEM((TOK, HD), F32),
            pltpu.VMEM((TOK, HD), F32),
        ],
        compiler_params=pltpu.CompilerParams(vmem_limit_bytes=VLIM),
        name="attention",
    )(meta, qpos, qspan, kpos, kspan, *q, *g, *kv)
    return out[0:4], out[4:8], out[8:24]


def project_kernel(y_ref, w_ref, *rest):
    dq, dkv = rest[0:4], rest[4:8]
    band_ref, text_ref = rest[8:]
    y = y_ref[0]
    total = jnp.zeros(band_ref.shape, F32)
    for s in range(4):
        head = lax.rem(y + 4 - s, 4)
        w = w_ref[head]
        total = total + dot_nt(dq[s][TXT:, :], w[:, :HD]) + dot_nt(dkv[s][TXT:, :], w[:, HD:])
        text_ref[head, :, :HD] = dq[s][:TXT, :]
        text_ref[head, :, HD:] = dkv[s][:TXT, :]
    band_ref[...] = total.astype(BF)


def project(y, w_heads, dq, dkv):
    channels = w_heads.shape[1]
    return pl.pallas_call(
        project_kernel,
        out_shape=[jax.ShapeDtypeStruct((IMG, channels), BF), jax.ShapeDtypeStruct((4, TXT, 3 * HD), BF)],
        in_specs=[smem()] + [vmem()] * 9,
        out_specs=[vmem()] * 2,
        compiler_params=pltpu.CompilerParams(vmem_limit_bytes=VLIM),
        name="project",
    )(y, w_heads, *dq, *dkv)


def slope_kernel(eg_ref, features_ref, conv_ref, out_ref):
    wide = eg_ref[...].astype(F32)
    total = jnp.zeros(out_ref.shape, F32)
    for a in range(3):
        for b in range(3):
            window = wide[2 - a : 6 - a, 2 - b : 10 - b, :].reshape(out_ref.shape).astype(BF)
            total = total + dot_nt(window, conv_ref[a, b])
    value = features_ref[...].astype(F32)
    sigma = 1.0 / (1.0 + jnp.exp(-value))
    slope = sigma * (1.0 + value * (1.0 - sigma))
    center = wide[1:5, 1:9, :].reshape(out_ref.shape)
    out_ref[...] = (center + slope * total).astype(BF)


def slope(eg, features, conv_weight):
    return pl.pallas_call(
        slope_kernel,
        out_shape=jax.ShapeDtypeStruct(features.shape, BF),
        in_specs=[vmem()] * 3,
        out_specs=vmem(),
        compiler_params=pltpu.CompilerParams(vmem_limit_bytes=VLIM),
        name="slope",
    )(eg, features, conv_weight)


def local(features, conv_weight, w_query_key, w_value, text_qkv, span_ids, out_cot):
    seq = lax.axis_index("seq")
    y, j = seq // 4, seq % 4
    rows, columns, channels = features.shape
    up = [(i, i + 1) for i in range(15)]
    down = [(i + 1, i) for i in range(15)]
    shift_y = [[(i, (i + 4 * s) % 16) for i in range(16)] for s in range(4)]
    swap_core = [(i, i ^ 1) for i in range(16)]
    swap_x = [(i, i ^ 2) for i in range(16)]

    def spread(pieces):
        return [pieces[0]] + [lax.ppermute(pieces[s], "seq", shift_y[s]) for s in (1, 2, 3)]

    spans = span_ids.reshape(16, TOK)
    offsets = jnp.arange(TOK, dtype=jnp.int32)
    first = jnp.min(jnp.where(spans >= 0, offsets[None, :], TOK), axis=1)
    span = jnp.max(spans, axis=1)
    order = jnp.where(
        offsets[None, :] >= TXT,
        first[:, None] + offsets[None, :] - TXT,
        jnp.where(offsets[None, :] < first[:, None], offsets[None, :], offsets[None, :] + IMG),
    )
    pos = order + TOK * jnp.arange(16, dtype=jnp.int32)[:, None]
    kspan = jnp.where(offsets[None, :] >= TXT, span[:, None], -1)
    qspan = jnp.where(offsets[None, :] >= TXT, span[:, None], -2)
    groups = 4 * jnp.arange(4, dtype=jnp.int32)
    of_query = groups + j
    of_key = (groups[:, None] + (j ^ jnp.arange(4, dtype=jnp.int32))[None, :]).reshape(-1)
    qpos_here = jnp.take(pos, of_query, axis=0)[:, :, None]
    qspan_here = jnp.take(qspan, of_query, axis=0)[:, :, None]
    kpos_here = jnp.take(pos, of_key, axis=0).reshape(4, 1, GRP)
    kspan_here = jnp.take(kspan, of_key, axis=0).reshape(4, 1, GRP)
    joined = (spans[:-1, -1] >= 0) & (spans[:-1, -1] == spans[1:, 0])
    joined = jnp.concatenate([joined, jnp.zeros((1,), jnp.bool_)]).reshape(4, 4)[:, 3] & (j == 3)
    y_arg = y.astype(jnp.int32).reshape(1)
    meta = jnp.concatenate([y_arg, joined.astype(jnp.int32)])
    own_order = lax.dynamic_index_in_dim(order, seq, 0, keepdims=False)
    to_stacked = (own_order[:, None] == offsets[None, :]).astype(BF)

    above = lax.ppermute(features[rows - 1 :], "seq", up)
    below = lax.ppermute(features[:1], "seq", down)
    tall = jnp.concatenate([above, features, below], axis=0)
    copies = jnp.broadcast_to(tall[None], (8,) + tall.shape)
    band = lax.all_to_all(copies, "col", 0, 0, tiled=True)
    band = jnp.transpose(band, (1, 0, 2, 3)).reshape((rows + 2) * 64, channels)

    cot = dot_nn(to_stacked, out_cot).astype(BF)
    cot = jnp.stack([cot[:, h * HD : (h + 1) * HD] for h in range(4)])
    g_send = [lax.dynamic_index_in_dim(cot, (y + s) % 4, 0, keepdims=False) for s in range(4)]
    g = spread(g_send)
    w_heads = jnp.concatenate([w_query_key, w_value[:, None]], axis=1).reshape(channels, 3, 4, HD)
    w_heads = jnp.transpose(w_heads, (2, 0, 1, 3)).reshape(4, channels, 3 * HD)
    text_heads = jnp.transpose(text_qkv.reshape(TXT, 3, 4, HD), (2, 0, 1, 3)).reshape(4, TXT, 3 * HD)

    out = encode(y_arg, band, conv_weight, w_heads, text_heads)
    kv_own = spread(out[:4])
    q = spread(out[4:])
    kv_x = [lax.ppermute(piece, "seq", swap_x) for piece in kv_own]
    kv_core = [lax.ppermute(piece, "seq", swap_core) for piece in kv_own]
    kv_x_core = [lax.ppermute(piece, "seq", swap_core) for piece in kv_x]
    att, dq, dkv = attention(
        meta, qpos_here, qspan_here, kpos_here, kspan_here, q, g, kv_own + kv_core + kv_x + kv_x_core
    )

    def add(mine, theirs):
        return (mine.astype(F32) + theirs.astype(F32)).astype(BF)

    def back(pieces):
        return [pieces[0]] + [lax.ppermute(pieces[s], "seq", shift_y[4 - s]) for s in (1, 2, 3)]

    far = [add(dkv[8 + s], lax.ppermute(dkv[12 + s], "seq", swap_core)) for s in range(4)]
    near = [add(dkv[s], lax.ppermute(dkv[4 + s], "seq", swap_core)) for s in range(4)]
    dkv_sum = [add(near[s], lax.ppermute(far[s], "seq", swap_x)) for s in range(4)]
    dq_back = back(dq)
    dkv_back = back(dkv_sum)
    att_back = back(att)
    turned = [0, 3, 2, 1]
    share, text_grad = project(y_arg, w_heads, [dq_back[t] for t in turned], [dkv_back[t] for t in turned])
    text_grad = jnp.transpose(text_grad.reshape(4, TXT, 3, HD), (1, 2, 0, 3)).reshape(TXT, 3, 4 * HD)
    att_heads = jnp.stack([att_back[t] for t in turned])
    att_heads = jnp.take(att_heads, (y - jnp.arange(4, dtype=jnp.int32)) % 4, axis=0)
    att_rows = jnp.transpose(att_heads, (1, 0, 2)).reshape(TOK, 4 * HD)
    attended = lax.dot_general(to_stacked, att_rows, (((0,), (0,)), ((), ())), preferred_element_type=F32).astype(BF)

    wide = jnp.pad(share.reshape(rows, 64, channels), ((0, 0), (1, 1), (0, 0)))
    parts = jnp.stack([wide[:, 8 * i : 8 * i + 10] for i in range(8)])
    parts = lax.all_to_all(parts, "col", 0, 0, tiled=True)
    eg = jnp.sum(parts.astype(F32), axis=0).astype(BF)
    eg_above = lax.ppermute(eg[rows - 1 :], "seq", up)
    eg_below = lax.ppermute(eg[:1], "seq", down)
    eg = jnp.concatenate([eg_above, eg, eg_below], axis=0)
    feature_grad = slope(eg, features.reshape(rows * columns, channels), conv_weight)
    return (attended, feature_grad.reshape(features.shape), text_grad)


def solution(mesh):
    in_specs = (
        P("seq", "col", None),
        P(),
        P(None, None, "col"),
        P(None, "col"),
        P("seq", None, "col"),
        P(),
        P("seq", "col"),
    )
    out_specs = (P("seq", "col"), P("seq", "col", None), P("seq", None, "col"))
    return jax.shard_map(local, mesh=mesh, in_specs=in_specs, out_specs=out_specs, check_vma=False)
```

```python
import functools
import math

import jax
import jax.numpy as jnp
from jax import lax
from jax.experimental import pallas as pl
from jax.experimental.pallas import tpu as pltpu
from jax.sharding import PartitionSpec as P

HD = 128
TXT = 64
IMG = 256
TOK = 320
HALF = 2 * TOK
ORDER = (1, 3, 2, 0)
SCALE = HD ** -0.5
SCALE2 = SCALE * math.log2(math.e)
NEG = -1e30
BF = jnp.bfloat16
F32 = jnp.float32
MIB = 1024 * 1024


def dot_nt(a, b):
    return lax.dot_general(a, b, (((1,), (1,)), ((), ())), preferred_element_type=F32)


def dot_nn(a, b):
    return lax.dot_general(a, b, (((1,), (0,)), ((), ())), preferred_element_type=F32)


def vmem():
    return pl.BlockSpec(memory_space=pltpu.VMEM)


def smem():
    return pl.BlockSpec(memory_space=pltpu.SMEM)


def lanes(x, width):
    return jnp.concatenate([x] * (width // HD), axis=1)


def row_places(meta_ref, block, index):
    first = meta_ref[8 + block]
    text = jnp.where(index < first, index, index + IMG)
    place = jnp.where(index >= TXT, first + index - TXT, text)
    return place, index >= TXT


def turn_kernel(meta_ref, cot_ref, *g_refs):
    y = meta_ref[0]
    place, _ = row_places(meta_ref, 4 * y + meta_ref[1], lax.broadcasted_iota(jnp.int32, (TOK, TOK), 0))
    order = (place == lax.broadcasted_iota(jnp.int32, (TOK, TOK), 1)).astype(BF)
    for s in range(4):
        at = pl.ds(pl.multiple_of(lax.rem(y + s, 4) * HD, HD), HD)
        g_refs[s][...] = dot_nn(order, cot_ref[:, at]).astype(BF)


def turn(meta, cot):
    return pl.pallas_call(
        turn_kernel,
        out_shape=[jax.ShapeDtypeStruct((TOK, HD), BF)] * 4,
        in_specs=[smem(), vmem()],
        out_specs=[vmem()] * 4,
        compiler_params=pltpu.CompilerParams(vmem_limit_bytes=8 * MIB),
        name="turn",
    )(meta, cot)


def tap_copies(conv_ref, taps_ref, sems):
    return [
        pltpu.make_async_copy(conv_ref.at[i // 3, i % 3], taps_ref.at[i], sems.at[i]) for i in range(9)
    ]


def tap_scratch(channels):
    return [pltpu.VMEM((9, channels, channels), BF), pltpu.SemaphoreType.DMA((9,))]


def encode_kernel(meta_ref, band_ref, conv_ref, wqk_ref, wv_ref, text_ref, *rest):
    kv_refs, q_refs = rest[:4], rest[4:8]
    act_ref, wide_ref, acc_ref, taps_ref, sems = rest[8:]
    copies = tap_copies(conv_ref, taps_ref, sems)
    for copy in copies:
        copy.start()
    rows = act_ref.shape[1]
    cells = rows - 2 * 64
    y = meta_ref[0]
    for r in range(6):
        for c in range(8):
            at = r * 64 + c * 8
            wide_ref[at : at + 8, :] = band_ref[c, r].astype(F32)
    wide = wide_ref[...]
    act = (wide / (1.0 + jnp.exp(-wide))).astype(BF).astype(F32)
    column = lax.broadcasted_iota(jnp.int32, act.shape, 0) % 64
    act_ref[0] = jnp.where(column == 0, 0.0, pltpu.roll(act, 1, 0)).astype(BF)
    act_ref[1] = act.astype(BF)
    act_ref[2] = jnp.where(column == 63, 0.0, pltpu.roll(act, rows - 1, 0)).astype(BF)
    acc_ref[...] = wide_ref[64 : 64 + cells, :]
    for a in range(3):
        total = acc_ref[...]
        for b in range(3):
            copies[3 * a + b].wait()
            total = total + dot_nn(act_ref[b, a * 64 : a * 64 + cells, :], taps_ref[3 * a + b])
        acc_ref[...] = total
    encoded = acc_ref[...].astype(BF)
    for s in range(4):
        head = lax.rem(y + s, 4)
        at = [pl.ds(pl.multiple_of((4 * i + head) * HD, HD), HD) for i in range(3)]
        w = jnp.concatenate([wqk_ref[:, at[0]], wqk_ref[:, at[1]], wv_ref[:, at[0]]], axis=1)
        qkv = dot_nn(encoded, w).astype(BF)
        q_refs[s][:TXT, :] = text_ref[:, at[0]]
        q_refs[s][TXT:, :] = qkv[:, :HD]
        kv_refs[s][:TXT, :HD] = text_ref[:, at[1]]
        kv_refs[s][:TXT, HD:] = text_ref[:, at[2]]
        kv_refs[s][TXT:, :] = qkv[:, HD:]


def anywhere():
    return pl.BlockSpec(memory_space=pl.ANY)


def encode(meta, band, conv_weight, w_qk, w_v, text):
    channels = band.shape[3]
    tall = 6 * 64
    return pl.pallas_call(
        encode_kernel,
        out_shape=[jax.ShapeDtypeStruct((TOK, 2 * HD), BF)] * 4 + [jax.ShapeDtypeStruct((TOK, HD), BF)] * 4,
        in_specs=[smem(), vmem(), anywhere()] + [vmem()] * 3,
        out_specs=[vmem()] * 8,
        scratch_shapes=[
            pltpu.VMEM((3, tall, channels), BF),
            pltpu.VMEM((tall, channels), F32),
            pltpu.VMEM((tall - 128, channels), F32),
        ]
        + tap_scratch(channels),
        compiler_params=pltpu.CompilerParams(vmem_limit_bytes=60 * MIB),
        name="encode",
    )(meta, band, conv_weight, w_qk, w_v, text)


def half_setup(meta_ref, rels, kv, k_ref, v_ref, kpos_ref, kspan_ref):
    y, j = meta_ref[0], meta_ref[1]
    for s in range(4):
        group = lax.rem(y + 4 - s, 4)
        for i in range(2):
            at = pl.ds(pl.multiple_of(group * HALF + i * TOK, 64), TOK)
            piece, first = (kv[2 * i + 1], ORDER.index(s) * TOK) if s else (kv[2 * i], 0)
            k_ref[at, :] = piece[first : first + TOK, :HD]
            v_ref[at, :] = piece[first : first + TOK, HD:]
    for group in range(4):
        for i, rel in enumerate(rels):
            at = slice(group * HALF + i * TOK, group * HALF + (i + 1) * TOK)
            block = 4 * group + (j ^ rel)
            place, image = row_places(meta_ref, block, lax.broadcasted_iota(jnp.int32, (8, TOK), 1))
            kpos_ref[:, at] = place + TOK * block
            kspan_ref[:, at] = jnp.where(image, meta_ref[24 + block], -1)


def visible(meta_ref, slot, at, kpos_ref, kspan_ref):
    block = 4 * slot + meta_ref[1]
    place, image = row_places(meta_ref, block, lax.broadcasted_iota(jnp.int32, (TOK, HALF), 0))
    span = jnp.where(image, meta_ref[24 + block], -2)
    return (kpos_ref[:1, at] <= place + TOK * block) | (kspan_ref[:1, at] == span)


def each_slot(meta_ref, rels, update):
    for slot in range(4):
        update(slot, ([(0, slot * HALF, False)] if slot else []) + [(slot * HALF, (slot + 1) * HALF, True)])
        if 3 in rels and slot < 3:

            @pl.when(meta_ref[2 + slot] > 0)
            def _(slot=slot):
                update(slot, [((slot + 1) * HALF, (slot + 2) * HALF, True)])


def forward_kernel(rels, meta_ref, *rest):
    far = 3 in rels
    n_in = 5 if far else 8
    q_in, kv_in, rest = rest[:n_in], rest[n_in : n_in + 4], rest[n_in + 4 :]
    k_ref, v_ref, kpos_ref, kspan_ref = rest[-4:]
    y = meta_ref[0]
    if far:
        q_ref, g_ref = q_in[:2]
        att_out, (lse_ref, delta_ref), (m_ref, l_ref, o_ref) = rest[:4], rest[4:6], rest[6:9]
        for mine, given in zip((m_ref, l_ref, o_ref), q_in[2:]):
            mine[...] = given[...]
    else:
        q_ref, g_ref, m_ref, l_ref, o_ref = rest[:5]
        for s in range(4):
            slot = lax.rem(y + 4 - s, 4)
            q_ref[slot] = q_in[s][...]
            g_ref[slot] = q_in[4 + s][...]
    half_setup(meta_ref, rels, kv_in, k_ref, v_ref, kpos_ref, kspan_ref)

    def update(slot, ranges):
        parts, top = [], None
        for lo, hi, masked in ranges:
            scores = dot_nt(q_ref[slot], k_ref[lo:hi, :])
            if masked:
                scores = jnp.where(visible(meta_ref, slot, slice(lo, hi), kpos_ref, kspan_ref), scores, NEG)
            for c in range(0, hi - lo, HD):
                piece = scores[:, c : c + HD]
                top = piece if top is None else jnp.maximum(top, piece)
            parts.append(scores)
        new = jnp.broadcast_to(jnp.max(top, axis=1, keepdims=True) * SCALE2, (TOK, HD))
        mass, out = None, None
        if far:
            old = m_ref[slot]
            new = jnp.maximum(old, new)
            fade = jnp.exp2(old - new)
            mass, out = l_ref[slot] * fade, o_ref[slot] * fade
        m_ref[slot] = new
        for (lo, hi, masked), scores in zip(ranges, parts):
            weights = jnp.exp2(scores * SCALE2 - lanes(new, hi - lo))
            for c in range(0, hi - lo, HD):
                piece = weights[:, c : c + HD]
                mass = piece if mass is None else mass + piece
            term = dot_nn(weights.astype(BF), v_ref[lo:hi, :])
            out = term if out is None else out + term
        l_ref[slot] = mass
        o_ref[slot] = out

    each_slot(meta_ref, rels, update)

    if far:
        for s in range(4):
            slot = lax.rem(y + 4 - s, 4)
            mass = jnp.sum(l_ref[slot], axis=1, keepdims=True)
            attended = (o_ref[slot] * (1.0 / mass)).astype(BF)
            att_out[s][...] = attended
            lse_ref[slot] = m_ref[slot] + jnp.log2(mass)
            delta = jnp.sum(g_ref[slot].astype(F32) * attended.astype(F32), axis=1, keepdims=True)
            delta_ref[slot] = jnp.broadcast_to(delta, (TOK, HD))


WIDE = jax.ShapeDtypeStruct((4, TOK, HD), F32)
TALL = jax.ShapeDtypeStruct((4, TOK, HD), BF)
NARROW = jax.ShapeDtypeStruct((TOK, HD), BF)


def half_scratch():
    return [
        pltpu.VMEM((4 * HALF, HD), BF),
        pltpu.VMEM((4 * HALF, HD), BF),
        pltpu.VMEM((8, 4 * HALF), jnp.int32),
        pltpu.VMEM((8, 4 * HALF), jnp.int32),
    ]


def cost(dots):
    flops = dots * 10 * 2 * TOK * HALF * HD
    return pl.CostEstimate(flops=flops, bytes_accessed=8 * MIB, transcendentals=10 * TOK * HALF)


def forward(rels, meta, q, kv):
    far = 3 in rels
    out_shape = [NARROW] * 4 + [WIDE] * 2 if far else [TALL] * 2 + [WIDE] * 3
    return pl.pallas_call(
        functools.partial(forward_kernel, rels),
        out_shape=out_shape,
        in_specs=[smem()] + [vmem()] * (len(q) + 4),
        out_specs=[vmem()] * len(out_shape),
        scratch_shapes=([pltpu.VMEM((4, TOK, HD), F32)] * 3 if far else []) + half_scratch(),
        compiler_params=pltpu.CompilerParams(vmem_limit_bytes=32 * MIB),
        cost_estimate=cost(2),
        name="forward_far" if far else "forward_near",
    )(meta, *q, *kv)


def backward_kernel(rels, meta_ref, q_ref, g_ref, lse_ref, delta_ref, *rest):
    far = 3 in rels
    if not far:
        dq_in, rest = rest[0], rest[1:]
    kv_in, rest = rest[:4], rest[4:]
    dq_out, (keep_ref, send_ref) = rest[: 1 if far else 4], rest[-11:-9]
    k_ref, v_ref, kpos_ref, kspan_ref, qt_ref, gt_ref, dk_ref, dv_ref, dq_ref = rest[-9:]
    y = meta_ref[0]
    dq_ref[...] = jnp.zeros_like(dq_ref) if far else dq_in[...]
    for slot in range(4):
        qt_ref[slot] = q_ref[slot].T
        gt_ref[slot] = g_ref[slot].T

    def update(slot, ranges):
        q, g = q_ref[slot], g_ref[slot]
        dq = dq_ref[slot]
        for lo, hi, masked in ranges:
            k, v = k_ref[lo:hi, :], v_ref[lo:hi, :]
            probs = jnp.exp2(dot_nt(q, k) * SCALE2 - lanes(lse_ref[slot], hi - lo))
            if masked:
                probs = jnp.where(visible(meta_ref, slot, slice(lo, hi), kpos_ref, kspan_ref), probs, 0.0)
            score_grad = (probs * (dot_nt(g, v) - lanes(delta_ref[slot], hi - lo))).astype(BF)
            dq = dq + dot_nn(score_grad, k)
            dk_ref[:, lo:hi] += dot_nn(qt_ref[slot], score_grad)
            dv_ref[:, lo:hi] += dot_nn(gt_ref[slot], probs.astype(BF))
        dq_ref[slot] = dq

    half_setup(meta_ref, rels, kv_in, k_ref, v_ref, kpos_ref, kspan_ref)
    dk_ref[...] = jnp.zeros_like(dk_ref)
    dv_ref[...] = jnp.zeros_like(dv_ref)
    each_slot(meta_ref, rels, update)
    for i, s in enumerate(ORDER):
        group = lax.rem(y + 4 - s, 4)
        of = pl.ds(pl.multiple_of(group * HALF, HD), HALF)
        key_grad = (dk_ref[:, of] * SCALE).T.astype(BF)
        value_grad = dv_ref[:, of].T.astype(BF)
        at = slice(i * TOK, (i + 1) * TOK)
        keep_ref[at, :HD] = key_grad[:TOK]
        keep_ref[at, HD:] = value_grad[:TOK]
        send_ref[at, :HD] = key_grad[TOK:]
        send_ref[at, HD:] = value_grad[TOK:]
    if far:
        dq_out[0][...] = dq_ref[...]
    else:
        for s in range(4):
            dq_out[s][...] = (dq_ref[lax.rem(y + 4 - s, 4)] * SCALE).astype(BF)


def backward(rels, meta, stats, dq, kv):
    far = 3 in rels
    dq_shape = [WIDE] if far else [NARROW] * 4
    out = pl.pallas_call(
        functools.partial(backward_kernel, rels),
        out_shape=dq_shape + [jax.ShapeDtypeStruct((4 * TOK, 2 * HD), BF)] * 2,
        in_specs=[smem()] + [vmem()] * (4 + len(dq) + 4),
        out_specs=[vmem()] * (len(dq_shape) + 2),
        scratch_shapes=half_scratch()
        + [
            pltpu.VMEM((4, HD, TOK), BF),
            pltpu.VMEM((4, HD, TOK), BF),
            pltpu.VMEM((HD, 4 * HALF), F32),
            pltpu.VMEM((HD, 4 * HALF), F32),
            pltpu.VMEM((4, TOK, HD), F32),
        ],
        compiler_params=pltpu.CompilerParams(vmem_limit_bytes=32 * MIB),
        cost_estimate=cost(5),
        name="backward_far" if far else "backward_near",
    )(meta, *stats, *dq, *kv)
    return out[: len(dq_shape)], out[-2], out[-1]


def merge_kernel(rows, with_att, near_ref, recv_ref, far_ref, *rest):
    n = len(rows)
    dq, att, outs = rest[:n], rest[n : 2 * n] if with_att else (), rest[-n:]
    for i, row in enumerate(rows):
        at = slice(row * TOK, (row + 1) * TOK)
        total = near_ref[at, :].astype(F32) + recv_ref[at, :].astype(F32)
        total = total + far_ref[i * TOK : (i + 1) * TOK, :].astype(F32)
        outs[i][:, :HD] = dq[i][...]
        outs[i][:, HD : 3 * HD] = total.astype(BF)
        if with_att:
            outs[i][:, 3 * HD :] = att[i][...]


def merge(rows, near, recv, far, dq, att):
    width = 4 * HD if att else 3 * HD
    return pl.pallas_call(
        functools.partial(merge_kernel, rows, bool(att)),
        out_shape=[jax.ShapeDtypeStruct((TOK, width), BF)] * len(rows),
        in_specs=[vmem()] * (3 + len(dq) + len(att)),
        out_specs=[vmem()] * len(rows),
        compiler_params=pltpu.CompilerParams(vmem_limit_bytes=12 * MIB),
        name="merge",
    )(near, recv, far, *dq, *att)


def project_kernel(meta_ref, wqk_ref, wv_ref, *rest):
    pieces, att = rest[0:4], rest[4:6]
    parts_ref, text_ref, att_ref = rest[6:9]
    wide_ref, cut_ref, order_ref = rest[9:]
    y = meta_ref[0]
    place, _ = row_places(meta_ref, 4 * y + meta_ref[1], lax.broadcasted_iota(jnp.int32, (TOK, TOK), 1))
    order_ref[...] = (place == lax.broadcasted_iota(jnp.int32, (TOK, TOK), 0)).astype(BF)
    total = jnp.zeros((IMG, wqk_ref.shape[0]), F32)
    for s in range(4):
        head = lax.rem(y + 4 - s, 4)
        at = [pl.ds(pl.multiple_of((4 * i + head) * HD, HD), HD) for i in range(3)]
        w = jnp.concatenate([wqk_ref[:, at[0]], wqk_ref[:, at[1]], wv_ref[:, at[0]]], axis=1)
        grads = pieces[s][:, : 3 * HD]
        total = total + dot_nt(grads[TXT:, :], w)
        for i in range(3):
            text_ref[i, :, at[0]] = grads[:TXT, i * HD : (i + 1) * HD]
        rows = att[s // 2][...] if s % 2 == 0 else pieces[s][:, 3 * HD :]
        att_ref[:, at[0]] = dot_nn(order_ref[...], rows).astype(BF)
    wide_ref[...] = jnp.zeros_like(wide_ref)
    wide_ref[:, 8:72, :] = total.reshape(4, 64, total.shape[1])
    for c in range(8):
        for i in range(4):
            cut_ref[10 * i : 10 * i + 10, :] = wide_ref[i, 8 * c + 7 : 8 * c + 17, :]
        parts_ref[c] = cut_ref[...].astype(BF)


def project(meta, w_qk, w_v, pieces, att):
    channels = w_qk.shape[0]
    return pl.pallas_call(
        project_kernel,
        out_shape=[
            jax.ShapeDtypeStruct((8, 40, channels), BF),
            jax.ShapeDtypeStruct((3, TXT, 4 * HD), BF),
            jax.ShapeDtypeStruct((TOK, 4 * HD), BF),
        ],
        in_specs=[smem()] + [vmem()] * 8,
        out_specs=[vmem()] * 3,
        scratch_shapes=[pltpu.VMEM((4, 80, channels), F32), pltpu.VMEM((40, channels), F32), pltpu.VMEM((TOK, TOK), BF)],
        compiler_params=pltpu.CompilerParams(vmem_limit_bytes=16 * MIB),
        name="project",
    )(meta, w_qk, w_v, *pieces, *att)


def slope_kernel(above_ref, eg_ref, below_ref, features_ref, conv_ref, out_ref, wide_ref, taps_ref, sems):
    copies = tap_copies(conv_ref, taps_ref, sems)
    for copy in copies:
        copy.start()
    wide_ref[0, :10] = above_ref[...].astype(F32)
    for i in range(4):
        wide_ref[i + 1, :10] = eg_ref[...].astype(F32)[10 * i : 10 * i + 10]
    wide_ref[5, :10] = below_ref[...].astype(F32)
    value = features_ref[...].astype(F32)
    sigma = 1.0 / (1.0 + jnp.exp(-value))
    slope = sigma * (1.0 + value * (1.0 - sigma))
    total = jnp.zeros(out_ref.shape, F32)
    for a in range(3):
        for b in range(3):
            window = wide_ref[2 - a : 6 - a, 2 - b : 10 - b, :].reshape(out_ref.shape).astype(BF)
            copies[3 * a + b].wait()
            total = total + dot_nt(window, taps_ref[3 * a + b])
    center = wide_ref[1:5, 1:9, :].reshape(out_ref.shape)
    out_ref[...] = (center + slope * total).astype(BF)


def slope(above, eg, below, features, conv_weight):
    channels = features.shape[1]
    return pl.pallas_call(
        slope_kernel,
        out_shape=jax.ShapeDtypeStruct(features.shape, BF),
        in_specs=[vmem()] * 4 + [anywhere()],
        out_specs=vmem(),
        scratch_shapes=[pltpu.VMEM((6, 16, channels), F32)] + tap_scratch(channels),
        compiler_params=pltpu.CompilerParams(vmem_limit_bytes=60 * MIB),
        name="slope",
    )(above, eg, below, features, conv_weight)


def local(features, conv_weight, w_query_key, w_value, text_qkv, span_ids, out_cot):
    seq = lax.axis_index("seq")
    y, j = seq // 4, seq % 4
    rows, columns, channels = features.shape
    up = [(i, i + 1) for i in range(15)]
    down = [(i + 1, i) for i in range(15)]
    shift_y = [[(i, (i + 4 * s) % 16) for i in range(16)] for s in range(4)]
    swap_core = [(i, i ^ 1) for i in range(16)]
    swap_x = [(i, i ^ 2) for i in range(16)]

    above = lax.ppermute(features[rows - 1 :], "seq", up)
    below = lax.ppermute(features[:1], "seq", down)
    tall = jnp.concatenate([above, features, below], axis=0)
    copies = jnp.broadcast_to(tall[None], (8,) + tall.shape)
    band = lax.all_to_all(copies, "col", 0, 0, tiled=True)

    spans = span_ids.reshape(16, TOK)
    offsets = jnp.arange(TOK, dtype=jnp.int32)
    first = jnp.min(jnp.where(spans >= 0, offsets[None, :], TOK), axis=1)
    span = jnp.max(spans, axis=1)
    ends, starts = spans[3:15:4, -1], spans[4:16:4, 0]
    joined = (ends >= 0) & (ends == starts) & (j == 3)
    scalars = [jnp.stack([y, j]), joined, jnp.zeros((3,), jnp.int32), first, span]
    meta = jnp.concatenate([part.astype(jnp.int32) for part in scalars])

    w_qk = w_query_key.reshape(channels, 8 * HD)
    g = turn(meta, out_cot)
    g = [lax.ppermute(g[s], "seq", shift_y[s]) if s else g[0] for s in range(4)]
    band, g = lax.optimization_barrier((band, g))
    out = encode(meta, band, conv_weight, w_qk, w_value, text_qkv.reshape(TXT, 12 * HD))
    q = list(out[4:])
    own = [out[0], jnp.concatenate([lax.ppermute(out[s], "seq", shift_y[s]) for s in ORDER[:3]])]
    crossed = [lax.ppermute(own[0], "seq", swap_x)]
    q[1], q[2], q[3], own[1], crossed[0] = lax.optimization_barrier((q[1], q[2], q[3], own[1], crossed[0]))
    q = [lax.ppermute(q[s], "seq", shift_y[s]) if s else q[0] for s in range(4)]
    crossed.append(lax.ppermute(own[1], "seq", swap_x))
    near_kv = own + [lax.ppermute(piece, "seq", swap_core) for piece in own]
    q, g, *state = forward((0, 1), meta, q + g, near_kv)
    crossed, state = lax.optimization_barrier((crossed, state))
    far_kv = crossed + [lax.ppermute(piece, "seq", swap_core) for piece in crossed]
    *att, lse, delta = forward((2, 3), meta, [q, g, *state], far_kv)
    stats = [q, g, lse, delta]

    def back(piece, s):
        return lax.ppermute(piece, "seq", shift_y[4 - s])

    dq, keep, send = backward((2, 3), meta, stats, [], far_kv)
    far = (keep.astype(F32) + lax.ppermute(send, "seq", swap_core).astype(F32)).astype(BF)
    far, dq = lax.optimization_barrier((far, dq))
    far = [lax.ppermute(far[a * TOK : (a + 2) * TOK], "seq", swap_x) for a in (0, 2)]
    dq, keep, send = backward((0, 1), meta, stats, dq, near_kv)
    att2 = back(att[2], 2)
    far[0], dq, keep, send, att2 = lax.optimization_barrier((far[0], dq, keep, send, att2))
    recv = lax.ppermute(send, "seq", swap_core)
    piece1, piece3 = merge((0, 1), keep, recv, far[0], [dq[1], dq[3]], [att[1], att[3]])
    piece1, piece3 = back(piece1, 1), back(piece3, 3)
    piece2, piece0 = merge((2, 3), keep, recv, far[1], [dq[2], dq[0]], [])
    piece2 = back(piece2, 2)
    parts, text_grad, attended = project(
        meta, w_qk, w_value, [piece0, piece3, piece2, piece1], [att[0], att2]
    )
    text_grad = jnp.transpose(text_grad, (1, 0, 2))

    parts = lax.all_to_all(parts, "col", 0, 0, tiled=True)
    eg = jnp.sum(parts.astype(F32), axis=0).astype(BF)
    eg_above = lax.ppermute(eg[30:], "seq", up)
    eg_below = lax.ppermute(eg[:10], "seq", down)
    feature_grad = slope(eg_above, eg, eg_below, features.reshape(rows * columns, channels), conv_weight)
    return (attended, feature_grad.reshape(features.shape), text_grad)


def solution(mesh):
    in_specs = (
        P("seq", "col", None),
        P(),
        P(None, None, "col"),
        P(None, "col"),
        P("seq", None, "col"),
        P(),
        P("seq", "col"),
    )
    out_specs = (P("seq", "col"), P("seq", "col", None), P("seq", None, "col"))
    return jax.shard_map(local, mesh=mesh, in_specs=in_specs, out_specs=out_specs, check_vma=False)
```

```python
import functools
import math

import jax
import jax.numpy as jnp
from jax import lax
from jax.experimental import pallas as pl
from jax.experimental.pallas import tpu as pltpu
from jax.sharding import PartitionSpec as P

HD = 128
TXT = 64
IMG = 256
TOK = 320
HALF = 2 * TOK
ORDER = (1, 3, 2, 0)
SCALE = HD ** -0.5
SCALE2 = SCALE * math.log2(math.e)
NEG = -1e30
BF = jnp.bfloat16
F32 = jnp.float32
MIB = 1024 * 1024


def dot_nt(a, b):
    return lax.dot_general(a, b, (((1,), (1,)), ((), ())), preferred_element_type=F32)


def dot_nn(a, b):
    return lax.dot_general(a, b, (((1,), (0,)), ((), ())), preferred_element_type=F32)


def vmem():
    return pl.BlockSpec(memory_space=pltpu.VMEM)


def smem():
    return pl.BlockSpec(memory_space=pltpu.SMEM)


def lanes(x, width):
    return jnp.concatenate([x] * (width // HD), axis=1)


def row_places(meta_ref, block, index):
    first = meta_ref[8 + block]
    text = jnp.where(index < first, index, index + IMG)
    place = jnp.where(index >= TXT, first + index - TXT, text)
    return place, index >= TXT


def turn_kernel(meta_ref, cot_ref, *g_refs):
    y = meta_ref[0]
    place, _ = row_places(meta_ref, 4 * y + meta_ref[1], lax.broadcasted_iota(jnp.int32, (TOK, TOK), 0))
    order = (place == lax.broadcasted_iota(jnp.int32, (TOK, TOK), 1)).astype(BF)
    for s in range(4):
        at = pl.ds(pl.multiple_of(lax.rem(y + s, 4) * HD, HD), HD)
        g_refs[s][...] = dot_nn(order, cot_ref[:, at]).astype(BF)


def turn(meta, cot):
    return pl.pallas_call(
        turn_kernel,
        out_shape=[jax.ShapeDtypeStruct((TOK, HD), BF)] * 4,
        in_specs=[smem(), vmem()],
        out_specs=[vmem()] * 4,
        compiler_params=pltpu.CompilerParams(vmem_limit_bytes=8 * MIB),
        name="turn",
    )(meta, cot)


def stage_kernel(in_ref, out_ref, sems):
    copies = [
        pltpu.make_async_copy(in_ref.at[i // 3, i % 3], out_ref.at[i // 3, i % 3], sems.at[i]) for i in range(9)
    ]
    for copy in copies:
        copy.start()
    for copy in copies:
        copy.wait()


def stage(conv_weight, name):
    return pl.pallas_call(
        stage_kernel,
        out_shape=jax.ShapeDtypeStruct(conv_weight.shape, BF),
        in_specs=[pl.BlockSpec(memory_space=pltpu.HBM)],
        out_specs=vmem(),
        scratch_shapes=[pltpu.SemaphoreType.DMA((9,))],
        compiler_params=pltpu.CompilerParams(vmem_limit_bytes=8 * MIB),
        name=name,
    )(conv_weight)


def shifted_act(wide):
    cells = wide.shape[0]
    act = (wide / (1.0 + jnp.exp(-wide))).astype(BF).astype(F32)
    column = lax.broadcasted_iota(jnp.int32, act.shape, 0) % 64
    left = jnp.where(column == 0, 0.0, pltpu.roll(act, 1, 0)).astype(BF)
    right = jnp.where(column == 63, 0.0, pltpu.roll(act, cells - 1, 0)).astype(BF)
    return left, act.astype(BF), right


def inner_kernel(band_ref, conv_ref, acc_ref, act_ref):
    for r in range(4):
        for c in range(8):
            at = r * 64 + c * 8
            acc_ref[at : at + 8, :] = band_ref[c, r].astype(F32)
    wide = acc_ref[...]
    for b, act in enumerate(shifted_act(wide)):
        act_ref[b] = act
    cells = wide.shape[0]
    total = wide
    for b in range(3):
        total = total + dot_nn(act_ref[b], conv_ref[1, b])
    acc_ref[...] = total
    low = acc_ref[64:, :]
    for b in range(3):
        low = low + dot_nn(act_ref[b, : cells - 64, :], conv_ref[0, b])
    acc_ref[64:, :] = low
    high = acc_ref[: cells - 64, :]
    for b in range(3):
        high = high + dot_nn(act_ref[b, 64:, :], conv_ref[2, b])
    acc_ref[: cells - 64, :] = high


def inner(band, conv_weight):
    channels = band.shape[3]
    return pl.pallas_call(
        inner_kernel,
        out_shape=jax.ShapeDtypeStruct((IMG, channels), F32),
        in_specs=[vmem()] * 2,
        out_specs=vmem(),
        scratch_shapes=[pltpu.VMEM((3, IMG, channels), BF)],
        compiler_params=pltpu.CompilerParams(vmem_limit_bytes=16 * MIB),
        name="inner",
    )(band, conv_weight)


def encode_kernel(meta_ref, acc_ref, above_ref, below_ref, conv_ref, wqk_ref, wv_ref, text_ref, *rest):
    kv_refs, q_refs = rest[:4], rest[4:8]
    edge_ref, encoded_ref = rest[8:]
    y = meta_ref[0]
    cells = acc_ref.shape[0]
    encoded_ref[...] = acc_ref[...].astype(BF)
    for rows_ref, a, at in ((above_ref, 0, 0), (below_ref, 2, cells - 64)):
        for c in range(8):
            edge_ref[8 * c : 8 * c + 8, :] = rows_ref[c].astype(F32)
        total = acc_ref[at : at + 64, :]
        for b, act in enumerate(shifted_act(edge_ref[...])):
            total = total + dot_nn(act, conv_ref[a, b])
        encoded_ref[at : at + 64, :] = total.astype(BF)
    encoded = encoded_ref[...]
    for s in range(4):
        head = lax.rem(y + s, 4)
        at = [pl.ds(pl.multiple_of((4 * i + head) * HD, HD), HD) for i in range(3)]
        w = jnp.concatenate([wqk_ref[:, at[0]], wqk_ref[:, at[1]], wv_ref[:, at[0]]], axis=1)
        qkv = dot_nn(encoded, w).astype(BF)
        q_refs[s][:TXT, :] = text_ref[:, at[0]]
        q_refs[s][TXT:, :] = qkv[:, :HD]
        kv_refs[s][:TXT, :HD] = text_ref[:, at[1]]
        kv_refs[s][:TXT, HD:] = text_ref[:, at[2]]
        kv_refs[s][TXT:, :] = qkv[:, HD:]


def encode(meta, acc, above, below, conv_weight, w_qk, w_v, text):
    channels = acc.shape[1]
    return pl.pallas_call(
        encode_kernel,
        out_shape=[jax.ShapeDtypeStruct((TOK, 2 * HD), BF)] * 4 + [jax.ShapeDtypeStruct((TOK, HD), BF)] * 4,
        in_specs=[smem()] + [vmem()] * 7,
        out_specs=[vmem()] * 8,
        scratch_shapes=[pltpu.VMEM((64, channels), F32), pltpu.VMEM((IMG, channels), BF)],
        compiler_params=pltpu.CompilerParams(vmem_limit_bytes=16 * MIB),
        name="encode",
    )(meta, acc, above, below, conv_weight, w_qk, w_v, text)


def half_setup(meta_ref, rels, kv, k_ref, v_ref, kpos_ref, kspan_ref):
    y, j = meta_ref[0], meta_ref[1]
    for s in range(4):
        group = lax.rem(y + 4 - s, 4)
        for i in range(2):
            at = pl.ds(pl.multiple_of(group * HALF + i * TOK, 64), TOK)
            piece, first = (kv[2 * i + 1], ORDER.index(s) * TOK) if s else (kv[2 * i], 0)
            k_ref[at, :] = piece[first : first + TOK, :HD]
            v_ref[at, :] = piece[first : first + TOK, HD:]
    for group in range(4):
        for i, rel in enumerate(rels):
            at = slice(group * HALF + i * TOK, group * HALF + (i + 1) * TOK)
            block = 4 * group + (j ^ rel)
            place, image = row_places(meta_ref, block, lax.broadcasted_iota(jnp.int32, (8, TOK), 1))
            kpos_ref[:, at] = place + TOK * block
            kspan_ref[:, at] = jnp.where(image, meta_ref[24 + block], -1)


def visible(meta_ref, slot, at, kpos_ref, kspan_ref):
    block = 4 * slot + meta_ref[1]
    place, image = row_places(meta_ref, block, lax.broadcasted_iota(jnp.int32, (TOK, HALF), 0))
    span = jnp.where(image, meta_ref[24 + block], -2)
    return (kpos_ref[:1, at] <= place + TOK * block) | (kspan_ref[:1, at] == span)


def each_slot(meta_ref, rels, update):
    for slot in range(4):
        update(slot, ([(0, slot * HALF, False)] if slot else []) + [(slot * HALF, (slot + 1) * HALF, True)])
        if 3 in rels and slot < 3:

            @pl.when(meta_ref[2 + slot] > 0)
            def _(slot=slot):
                update(slot, [((slot + 1) * HALF, (slot + 2) * HALF, True)])


def forward_kernel(rels, meta_ref, *rest):
    far = 3 in rels
    n_in = 5 if far else 8
    q_in, kv_in, rest = rest[:n_in], rest[n_in : n_in + 4], rest[n_in + 4 :]
    k_ref, v_ref, kpos_ref, kspan_ref = rest[-4:]
    y = meta_ref[0]
    if far:
        q_ref, g_ref = q_in[:2]
        att_out, (lse_ref, delta_ref), (m_ref, l_ref, o_ref) = rest[:4], rest[4:6], rest[6:9]
        for mine, given in zip((m_ref, l_ref, o_ref), q_in[2:]):
            mine[...] = given[...]
    else:
        q_ref, g_ref, m_ref, l_ref, o_ref = rest[:5]
        for s in range(4):
            slot = lax.rem(y + 4 - s, 4)
            q_ref[slot] = q_in[s][...]
            g_ref[slot] = q_in[4 + s][...]
    half_setup(meta_ref, rels, kv_in, k_ref, v_ref, kpos_ref, kspan_ref)

    def update(slot, ranges):
        parts, top = [], None
        for lo, hi, masked in ranges:
            scores = dot_nt(q_ref[slot], k_ref[lo:hi, :])
            if masked:
                scores = jnp.where(visible(meta_ref, slot, slice(lo, hi), kpos_ref, kspan_ref), scores, NEG)
            for c in range(0, hi - lo, HD):
                piece = scores[:, c : c + HD]
                top = piece if top is None else jnp.maximum(top, piece)
            parts.append(scores)
        new = jnp.broadcast_to(jnp.max(top, axis=1, keepdims=True) * SCALE2, (TOK, HD))
        mass, out = None, None
        if far:
            old = m_ref[slot]
            new = jnp.maximum(old, new)
            fade = jnp.exp2(old - new)
            mass, out = l_ref[slot] * fade, o_ref[slot] * fade
        m_ref[slot] = new
        for (lo, hi, masked), scores in zip(ranges, parts):
            weights = jnp.exp2(scores * SCALE2 - lanes(new, hi - lo))
            for c in range(0, hi - lo, HD):
                piece = weights[:, c : c + HD]
                mass = piece if mass is None else mass + piece
            term = dot_nn(weights.astype(BF), v_ref[lo:hi, :])
            out = term if out is None else out + term
        l_ref[slot] = mass
        o_ref[slot] = out

    each_slot(meta_ref, rels, update)

    if far:
        for s in range(4):
            slot = lax.rem(y + 4 - s, 4)
            mass = jnp.sum(l_ref[slot], axis=1, keepdims=True)
            attended = (o_ref[slot] * (1.0 / mass)).astype(BF)
            att_out[s][...] = attended
            lse_ref[slot] = m_ref[slot] + jnp.log2(mass)
            delta = jnp.sum(g_ref[slot].astype(F32) * attended.astype(F32), axis=1, keepdims=True)
            delta_ref[slot] = jnp.broadcast_to(delta, (TOK, HD))


WIDE = jax.ShapeDtypeStruct((4, TOK, HD), F32)
TALL = jax.ShapeDtypeStruct((4, TOK, HD), BF)
NARROW = jax.ShapeDtypeStruct((TOK, HD), BF)


def half_scratch():
    return [
        pltpu.VMEM((4 * HALF, HD), BF),
        pltpu.VMEM((4 * HALF, HD), BF),
        pltpu.VMEM((8, 4 * HALF), jnp.int32),
        pltpu.VMEM((8, 4 * HALF), jnp.int32),
    ]


def cost(dots):
    flops = dots * 10 * 2 * TOK * HALF * HD
    return pl.CostEstimate(flops=flops, bytes_accessed=8 * MIB, transcendentals=10 * TOK * HALF)


def forward(rels, meta, q, kv):
    far = 3 in rels
    out_shape = [NARROW] * 4 + [WIDE] * 2 if far else [TALL] * 2 + [WIDE] * 3
    return pl.pallas_call(
        functools.partial(forward_kernel, rels),
        out_shape=out_shape,
        in_specs=[smem()] + [vmem()] * (len(q) + 4),
        out_specs=[vmem()] * len(out_shape),
        scratch_shapes=([pltpu.VMEM((4, TOK, HD), F32)] * 3 if far else []) + half_scratch(),
        compiler_params=pltpu.CompilerParams(vmem_limit_bytes=32 * MIB),
        cost_estimate=cost(2),
        name="forward_far" if far else "forward_near",
    )(meta, *q, *kv)


def backward_kernel(rels, meta_ref, q_ref, g_ref, lse_ref, delta_ref, *rest):
    far = 3 in rels
    if not far:
        dq_in, rest = rest[0], rest[1:]
    kv_in, rest = rest[:4], rest[4:]
    dq_out, (keep_ref, send_ref) = rest[: 1 if far else 4], rest[-11:-9]
    k_ref, v_ref, kpos_ref, kspan_ref, qt_ref, gt_ref, dk_ref, dv_ref, dq_ref = rest[-9:]
    y = meta_ref[0]
    dq_ref[...] = jnp.zeros_like(dq_ref) if far else dq_in[...]
    for slot in range(4):
        qt_ref[slot] = q_ref[slot].T
        gt_ref[slot] = g_ref[slot].T

    def update(slot, ranges):
        q, g = q_ref[slot], g_ref[slot]
        dq = dq_ref[slot]
        for lo, hi, masked in ranges:
            k, v = k_ref[lo:hi, :], v_ref[lo:hi, :]
            probs = jnp.exp2(dot_nt(q, k) * SCALE2 - lanes(lse_ref[slot], hi - lo))
            if masked:
                probs = jnp.where(visible(meta_ref, slot, slice(lo, hi), kpos_ref, kspan_ref), probs, 0.0)
            score_grad = (probs * (dot_nt(g, v) - lanes(delta_ref[slot], hi - lo))).astype(BF)
            dq = dq + dot_nn(score_grad, k)
            dk_ref[:, lo:hi] += dot_nn(qt_ref[slot], score_grad)
            dv_ref[:, lo:hi] += dot_nn(gt_ref[slot], probs.astype(BF))
        dq_ref[slot] = dq

    half_setup(meta_ref, rels, kv_in, k_ref, v_ref, kpos_ref, kspan_ref)
    dk_ref[...] = jnp.zeros_like(dk_ref)
    dv_ref[...] = jnp.zeros_like(dv_ref)
    each_slot(meta_ref, rels, update)
    for i, s in enumerate(ORDER):
        group = lax.rem(y + 4 - s, 4)
        of = pl.ds(pl.multiple_of(group * HALF, HD), HALF)
        key_grad = (dk_ref[:, of] * SCALE).T.astype(BF)
        value_grad = dv_ref[:, of].T.astype(BF)
        at = slice(i * TOK, (i + 1) * TOK)
        keep_ref[at, :HD] = key_grad[:TOK]
        keep_ref[at, HD:] = value_grad[:TOK]
        send_ref[at, :HD] = key_grad[TOK:]
        send_ref[at, HD:] = value_grad[TOK:]
    if far:
        dq_out[0][...] = dq_ref[...]
    else:
        for s in range(4):
            dq_out[s][...] = (dq_ref[lax.rem(y + 4 - s, 4)] * SCALE).astype(BF)


def backward(rels, meta, stats, dq, kv):
    far = 3 in rels
    dq_shape = [WIDE] if far else [NARROW] * 4
    out = pl.pallas_call(
        functools.partial(backward_kernel, rels),
        out_shape=dq_shape + [jax.ShapeDtypeStruct((4 * TOK, 2 * HD), BF)] * 2,
        in_specs=[smem()] + [vmem()] * (4 + len(dq) + 4),
        out_specs=[vmem()] * (len(dq_shape) + 2),
        scratch_shapes=half_scratch()
        + [
            pltpu.VMEM((4, HD, TOK), BF),
            pltpu.VMEM((4, HD, TOK), BF),
            pltpu.VMEM((HD, 4 * HALF), F32),
            pltpu.VMEM((HD, 4 * HALF), F32),
            pltpu.VMEM((4, TOK, HD), F32),
        ],
        compiler_params=pltpu.CompilerParams(vmem_limit_bytes=32 * MIB),
        cost_estimate=cost(5),
        name="backward_far" if far else "backward_near",
    )(meta, *stats, *dq, *kv)
    return out[: len(dq_shape)], out[-2], out[-1]


def merge_kernel(rows, with_att, near_ref, recv_ref, far_ref, *rest):
    n = len(rows)
    dq, att, outs = rest[:n], rest[n : 2 * n] if with_att else (), rest[-n:]
    for i, row in enumerate(rows):
        at = slice(row * TOK, (row + 1) * TOK)
        total = near_ref[at, :].astype(F32) + recv_ref[at, :].astype(F32)
        total = total + far_ref[i * TOK : (i + 1) * TOK, :].astype(F32)
        outs[i][:, :HD] = dq[i][...]
        outs[i][:, HD : 3 * HD] = total.astype(BF)
        if with_att:
            outs[i][:, 3 * HD :] = att[i][...]


def merge(rows, near, recv, far, dq, att):
    width = 4 * HD if att else 3 * HD
    return pl.pallas_call(
        functools.partial(merge_kernel, rows, bool(att)),
        out_shape=[jax.ShapeDtypeStruct((TOK, width), BF)] * len(rows),
        in_specs=[vmem()] * (3 + len(dq) + len(att)),
        out_specs=[vmem()] * len(rows),
        compiler_params=pltpu.CompilerParams(vmem_limit_bytes=12 * MIB),
        name="merge",
    )(near, recv, far, *dq, *att)


def project_kernel(meta_ref, wqk_ref, wv_ref, *rest):
    pieces, att = rest[0:4], rest[4:6]
    parts_ref, text_ref, att_ref = rest[6:9]
    wide_ref, cut_ref, order_ref = rest[9:]
    y = meta_ref[0]
    place, _ = row_places(meta_ref, 4 * y + meta_ref[1], lax.broadcasted_iota(jnp.int32, (TOK, TOK), 1))
    order_ref[...] = (place == lax.broadcasted_iota(jnp.int32, (TOK, TOK), 0)).astype(BF)
    total = jnp.zeros((IMG, wqk_ref.shape[0]), F32)
    for s in range(4):
        head = lax.rem(y + 4 - s, 4)
        at = [pl.ds(pl.multiple_of((4 * i + head) * HD, HD), HD) for i in range(3)]
        w = jnp.concatenate([wqk_ref[:, at[0]], wqk_ref[:, at[1]], wv_ref[:, at[0]]], axis=1)
        grads = pieces[s][:, : 3 * HD]
        total = total + dot_nt(grads[TXT:, :], w)
        for i in range(3):
            text_ref[i, :, at[0]] = grads[:TXT, i * HD : (i + 1) * HD]
        rows = att[s // 2][...] if s % 2 == 0 else pieces[s][:, 3 * HD :]
        att_ref[:, at[0]] = dot_nn(order_ref[...], rows).astype(BF)
    wide_ref[...] = jnp.zeros_like(wide_ref)
    wide_ref[:, 8:72, :] = total.reshape(4, 64, total.shape[1])
    for c in range(8):
        for i in range(4):
            cut_ref[10 * i : 10 * i + 10, :] = wide_ref[i, 8 * c + 7 : 8 * c + 17, :]
        parts_ref[c] = cut_ref[...].astype(BF)


def project(meta, w_qk, w_v, pieces, att):
    channels = w_qk.shape[0]
    return pl.pallas_call(
        project_kernel,
        out_shape=[
            jax.ShapeDtypeStruct((8, 40, channels), BF),
            jax.ShapeDtypeStruct((3, TXT, 4 * HD), BF),
            jax.ShapeDtypeStruct((TOK, 4 * HD), BF),
        ],
        in_specs=[smem()] + [vmem()] * 8,
        out_specs=[vmem()] * 3,
        scratch_shapes=[pltpu.VMEM((4, 80, channels), F32), pltpu.VMEM((40, channels), F32), pltpu.VMEM((TOK, TOK), BF)],
        compiler_params=pltpu.CompilerParams(vmem_limit_bytes=16 * MIB),
        name="project",
    )(meta, w_qk, w_v, *pieces, *att)


def slope_kernel(above_ref, eg_ref, below_ref, features_ref, conv_ref, out_ref, wide_ref):
    wide_ref[0, :10] = above_ref[...].astype(F32)
    for i in range(4):
        wide_ref[i + 1, :10] = eg_ref[...].astype(F32)[10 * i : 10 * i + 10]
    wide_ref[5, :10] = below_ref[...].astype(F32)
    value = features_ref[...].astype(F32)
    sigma = 1.0 / (1.0 + jnp.exp(-value))
    slope = sigma * (1.0 + value * (1.0 - sigma))
    total = jnp.zeros(out_ref.shape, F32)
    for a in range(3):
        for b in range(3):
            window = wide_ref[2 - a : 6 - a, 2 - b : 10 - b, :].reshape(out_ref.shape).astype(BF)
            total = total + dot_nt(window, conv_ref[a, b])
    center = wide_ref[1:5, 1:9, :].reshape(out_ref.shape)
    out_ref[...] = (center + slope * total).astype(BF)


def slope(above, eg, below, features, conv_weight):
    channels = features.shape[1]
    return pl.pallas_call(
        slope_kernel,
        out_shape=jax.ShapeDtypeStruct(features.shape, BF),
        in_specs=[vmem()] * 5,
        out_specs=vmem(),
        scratch_shapes=[pltpu.VMEM((6, 16, channels), F32)],
        compiler_params=pltpu.CompilerParams(vmem_limit_bytes=12 * MIB),
        name="slope",
    )(above, eg, below, features, conv_weight)


def local(features, conv_weight, w_query_key, w_value, text_qkv, span_ids, out_cot):
    seq = lax.axis_index("seq")
    y, j = seq // 4, seq % 4
    rows, columns, channels = features.shape
    up = [(i, i + 1) for i in range(15)]
    down = [(i + 1, i) for i in range(15)]
    shift_y = [[(i, (i + 4 * s) % 16) for i in range(16)] for s in range(4)]
    swap_core = [(i, i ^ 1) for i in range(16)]
    swap_x = [(i, i ^ 2) for i in range(16)]

    copies = jnp.broadcast_to(features[None], (8,) + features.shape)
    band = lax.all_to_all(copies, "col", 0, 0, tiled=True)
    above = lax.ppermute(band[:, rows - 1], "seq", up)
    below = lax.ppermute(band[:, 0], "seq", down)

    spans = span_ids.reshape(16, TOK)
    offsets = jnp.arange(TOK, dtype=jnp.int32)
    first = jnp.min(jnp.where(spans >= 0, offsets[None, :], TOK), axis=1)
    span = jnp.max(spans, axis=1)
    ends, starts = spans[3:15:4, -1], spans[4:16:4, 0]
    joined = (ends >= 0) & (ends == starts) & (j == 3)
    scalars = [jnp.stack([y, j]), joined, jnp.zeros((3,), jnp.int32), first, span]
    meta = jnp.concatenate([part.astype(jnp.int32) for part in scalars])

    w_qk = w_query_key.reshape(channels, 8 * HD)
    taps = stage(conv_weight, "stage")
    g = turn(meta, out_cot)
    g = [lax.ppermute(g[s], "seq", shift_y[s]) if s else g[0] for s in range(4)]
    acc = inner(band, taps)
    above, below, acc, g = lax.optimization_barrier((above, below, acc, g))
    out = encode(meta, acc, above, below, taps, w_qk, w_value, text_qkv.reshape(TXT, 12 * HD))
    q = list(out[4:])
    own = [out[0], jnp.concatenate([lax.ppermute(out[s], "seq", shift_y[s]) for s in ORDER[:3]])]
    crossed = [lax.ppermute(own[0], "seq", swap_x)]
    q[1], q[2], q[3], own[1], crossed[0] = lax.optimization_barrier((q[1], q[2], q[3], own[1], crossed[0]))
    q = [lax.ppermute(q[s], "seq", shift_y[s]) if s else q[0] for s in range(4)]
    crossed.append(lax.ppermute(own[1], "seq", swap_x))
    near_kv = own + [lax.ppermute(piece, "seq", swap_core) for piece in own]
    q, g, *state = forward((0, 1), meta, q + g, near_kv)
    crossed, state = lax.optimization_barrier((crossed, state))
    far_kv = crossed + [lax.ppermute(piece, "seq", swap_core) for piece in crossed]
    *att, lse, delta = forward((2, 3), meta, [q, g, *state], far_kv)
    stats = [q, g, lse, delta]

    def back(piece, s):
        return lax.ppermute(piece, "seq", shift_y[4 - s])

    dq, keep, send = backward((2, 3), meta, stats, [], far_kv)
    far = (keep.astype(F32) + lax.ppermute(send, "seq", swap_core).astype(F32)).astype(BF)
    far, dq = lax.optimization_barrier((far, dq))
    far = [lax.ppermute(far[a * TOK : (a + 2) * TOK], "seq", swap_x) for a in (0, 2)]
    dq, keep, send = backward((0, 1), meta, stats, dq, near_kv)
    att2 = back(att[2], 2)
    far[0], dq, keep, send, att2 = lax.optimization_barrier((far[0], dq, keep, send, att2))
    recv = lax.ppermute(send, "seq", swap_core)
    piece1, piece3 = merge((0, 1), keep, recv, far[0], [dq[1], dq[3]], [att[1], att[3]])
    piece1, piece3 = back(piece1, 1), back(piece3, 3)
    piece2, piece0 = merge((2, 3), keep, recv, far[1], [dq[2], dq[0]], [])
    piece2 = back(piece2, 2)
    parts, text_grad, attended = project(
        meta, w_qk, w_value, [piece0, piece3, piece2, piece1], [att[0], att2]
    )
    text_grad = jnp.transpose(text_grad, (1, 0, 2))

    conv_weight, parts = lax.optimization_barrier((conv_weight, parts))
    taps = stage(conv_weight, "stage_again")
    parts = lax.all_to_all(parts, "col", 0, 0, tiled=True)
    eg = jnp.sum(parts.astype(F32), axis=0).astype(BF)
    eg_above = lax.ppermute(eg[30:], "seq", up)
    eg_below = lax.ppermute(eg[:10], "seq", down)
    feature_grad = slope(eg_above, eg, eg_below, features.reshape(rows * columns, channels), taps)
    return (attended, feature_grad.reshape(features.shape), text_grad)


def solution(mesh):
    in_specs = (
        P("seq", "col", None),
        P(),
        P(None, None, "col"),
        P(None, "col"),
        P("seq", None, "col"),
        P(),
        P("seq", "col"),
    )
    out_specs = (P("seq", "col"), P("seq", "col", None), P("seq", None, "col"))
    return jax.shard_map(local, mesh=mesh, in_specs=in_specs, out_specs=out_specs, check_vma=False)
```

```python
import functools
import math

import jax
import jax.numpy as jnp
from jax import lax
from jax.experimental import pallas as pl
from jax.experimental.pallas import tpu as pltpu
from jax.sharding import PartitionSpec as P

HD = 128
TXT = 64
IMG = 256
TOK = 320
HALF = 2 * TOK
ORDER = (1, 3, 2, 0)
SCALE = HD ** -0.5
SCALE2 = SCALE * math.log2(math.e)
NEG = -1e30
BF = jnp.bfloat16
F32 = jnp.float32
MIB = 1024 * 1024


def dot_nt(a, b):
    return lax.dot_general(a, b, (((1,), (1,)), ((), ())), preferred_element_type=F32)


def dot_nn(a, b):
    return lax.dot_general(a, b, (((1,), (0,)), ((), ())), preferred_element_type=F32)


def vmem():
    return pl.BlockSpec(memory_space=pltpu.VMEM)


def smem():
    return pl.BlockSpec(memory_space=pltpu.SMEM)


def lanes(x, width):
    return jnp.concatenate([x] * (width // HD), axis=1)


def row_places(meta_ref, block, index):
    first = meta_ref[8 + block]
    text = jnp.where(index < first, index, index + IMG)
    place = jnp.where(index >= TXT, first + index - TXT, text)
    return place, index >= TXT


def turn_kernel(meta_ref, cot_ref, *g_refs):
    y = meta_ref[0]
    place, _ = row_places(meta_ref, 4 * y + meta_ref[1], lax.broadcasted_iota(jnp.int32, (TOK, TOK), 0))
    order = (place == lax.broadcasted_iota(jnp.int32, (TOK, TOK), 1)).astype(BF)
    for s in range(4):
        g_refs[s][...] = dot_nn(order, cot_ref[lax.rem(y + s, 4)]).astype(BF)


def turn(meta, cot):
    return pl.pallas_call(
        turn_kernel,
        out_shape=[jax.ShapeDtypeStruct((TOK, HD), BF)] * 4,
        in_specs=[smem(), vmem()],
        out_specs=[vmem()] * 4,
        compiler_params=pltpu.CompilerParams(vmem_limit_bytes=8 * MIB),
        name="turn",
    )(meta, cot)


def stage_kernel(in_ref, out_ref, sems):
    copies = [
        pltpu.make_async_copy(in_ref.at[i // 3, i % 3], out_ref.at[i // 3, i % 3], sems.at[i]) for i in range(9)
    ]
    for copy in copies:
        copy.start()
    for copy in copies:
        copy.wait()


def stage(conv_weight, name):
    return pl.pallas_call(
        stage_kernel,
        out_shape=jax.ShapeDtypeStruct(conv_weight.shape, BF),
        in_specs=[pl.BlockSpec(memory_space=pltpu.HBM)],
        out_specs=vmem(),
        scratch_shapes=[pltpu.SemaphoreType.DMA((9,))],
        compiler_params=pltpu.CompilerParams(vmem_limit_bytes=8 * MIB),
        name=name,
    )(conv_weight)


def shifted_act(wide):
    cells = wide.shape[0]
    act = (wide / (1.0 + jnp.exp(-wide))).astype(BF).astype(F32)
    column = lax.broadcasted_iota(jnp.int32, act.shape, 0) % 64
    left = jnp.where(column == 0, 0.0, pltpu.roll(act, 1, 0)).astype(BF)
    right = jnp.where(column == 63, 0.0, pltpu.roll(act, cells - 1, 0)).astype(BF)
    return left, act.astype(BF), right


def inner_kernel(band_ref, conv_ref, acc_ref, act_ref):
    for r in range(4):
        for c in range(8):
            at = r * 64 + c * 8
            acc_ref[at : at + 8, :] = band_ref[c, r].astype(F32)
    wide = acc_ref[...]
    for b, act in enumerate(shifted_act(wide)):
        act_ref[b] = act
    cells = wide.shape[0]
    total = wide
    for b in range(3):
        total = total + dot_nn(act_ref[b], conv_ref[1, b])
    acc_ref[...] = total
    low = acc_ref[64:, :]
    for b in range(3):
        low = low + dot_nn(act_ref[b, : cells - 64, :], conv_ref[0, b])
    acc_ref[64:, :] = low
    high = acc_ref[: cells - 64, :]
    for b in range(3):
        high = high + dot_nn(act_ref[b, 64:, :], conv_ref[2, b])
    acc_ref[: cells - 64, :] = high


def inner(band, conv_weight):
    channels = band.shape[3]
    return pl.pallas_call(
        inner_kernel,
        out_shape=jax.ShapeDtypeStruct((IMG, channels), F32),
        in_specs=[vmem()] * 2,
        out_specs=vmem(),
        scratch_shapes=[pltpu.VMEM((3, IMG, channels), BF)],
        compiler_params=pltpu.CompilerParams(vmem_limit_bytes=16 * MIB),
        name="inner",
    )(band, conv_weight)


def encode_kernel(meta_ref, acc_ref, above_ref, below_ref, conv_ref, wqk_ref, wv_ref, text_ref, *rest):
    kv_refs, q_refs = rest[:4], rest[4:8]
    edge_ref, encoded_ref = rest[8:]
    y = meta_ref[0]
    cells = acc_ref.shape[0]
    encoded_ref[...] = acc_ref[...].astype(BF)
    for rows_ref, a, at in ((above_ref, 0, 0), (below_ref, 2, cells - 64)):
        for c in range(8):
            edge_ref[8 * c : 8 * c + 8, :] = rows_ref[c].astype(F32)
        total = acc_ref[at : at + 64, :]
        for b, act in enumerate(shifted_act(edge_ref[...])):
            total = total + dot_nn(act, conv_ref[a, b])
        encoded_ref[at : at + 64, :] = total.astype(BF)
    encoded = encoded_ref[...]
    for s in range(4):
        head = lax.rem(y + s, 4)
        at = [pl.ds(pl.multiple_of((4 * i + head) * HD, HD), HD) for i in range(3)]
        w = jnp.concatenate([wqk_ref[:, at[0]], wqk_ref[:, at[1]], wv_ref[:, at[0]]], axis=1)
        qkv = dot_nn(encoded, w).astype(BF)
        q_refs[s][:TXT, :] = text_ref[:, at[0]]
        q_refs[s][TXT:, :] = qkv[:, :HD]
        kv_refs[s][:TXT, :HD] = text_ref[:, at[1]]
        kv_refs[s][:TXT, HD:] = text_ref[:, at[2]]
        kv_refs[s][TXT:, :] = qkv[:, HD:]


def encode(meta, acc, above, below, conv_weight, w_qk, w_v, text):
    channels = acc.shape[1]
    return pl.pallas_call(
        encode_kernel,
        out_shape=[jax.ShapeDtypeStruct((TOK, 2 * HD), BF)] * 4 + [jax.ShapeDtypeStruct((TOK, HD), BF)] * 4,
        in_specs=[smem()] + [vmem()] * 7,
        out_specs=[vmem()] * 8,
        scratch_shapes=[pltpu.VMEM((64, channels), F32), pltpu.VMEM((IMG, channels), BF)],
        compiler_params=pltpu.CompilerParams(vmem_limit_bytes=16 * MIB),
        name="encode",
    )(meta, acc, above, below, conv_weight, w_qk, w_v, text)


def half_setup(meta_ref, rels, kv, k_ref, v_ref, kpos_ref, kspan_ref):
    y, j = meta_ref[0], meta_ref[1]
    for s in range(4):
        group = lax.rem(y + 4 - s, 4)
        for i in range(2):
            at = pl.ds(pl.multiple_of(group * HALF + i * TOK, 64), TOK)
            piece, first = (kv[2 * i + 1], ORDER.index(s) * TOK) if s else (kv[2 * i], 0)
            k_ref[at, :] = piece[first : first + TOK, :HD]
            v_ref[at, :] = piece[first : first + TOK, HD:]
    for group in range(4):
        for i, rel in enumerate(rels):
            at = slice(group * HALF + i * TOK, group * HALF + (i + 1) * TOK)
            block = 4 * group + (j ^ rel)
            place, image = row_places(meta_ref, block, lax.broadcasted_iota(jnp.int32, (8, TOK), 1))
            kpos_ref[:, at] = place + TOK * block
            kspan_ref[:, at] = jnp.where(image, meta_ref[24 + block], -1)


def visible(meta_ref, slot, at, kpos_ref, kspan_ref):
    block = 4 * slot + meta_ref[1]
    place, image = row_places(meta_ref, block, lax.broadcasted_iota(jnp.int32, (TOK, HALF), 0))
    span = jnp.where(image, meta_ref[24 + block], -2)
    return (kpos_ref[:1, at] <= place + TOK * block) | (kspan_ref[:1, at] == span)


def each_slot(meta_ref, rels, update):
    for slot in range(4):
        update(slot, ([(0, slot * HALF, False)] if slot else []) + [(slot * HALF, (slot + 1) * HALF, True)])
        if 3 in rels and slot < 3:

            @pl.when(meta_ref[2 + slot] > 0)
            def _(slot=slot):
                update(slot, [((slot + 1) * HALF, (slot + 2) * HALF, True)])


def forward_kernel(rels, meta_ref, *rest):
    far = 3 in rels
    n_in = 5 if far else 8
    q_in, kv_in, rest = rest[:n_in], rest[n_in : n_in + 4], rest[n_in + 4 :]
    k_ref, v_ref, kpos_ref, kspan_ref = rest[-4:]
    y = meta_ref[0]
    if far:
        q_ref, g_ref = q_in[:2]
        att_out, (lse_ref, delta_ref), (m_ref, l_ref, o_ref) = rest[:4], rest[4:6], rest[6:9]
        for mine, given in zip((m_ref, l_ref, o_ref), q_in[2:]):
            mine[...] = given[...]
    else:
        q_ref, g_ref, m_ref, l_ref, o_ref = rest[:5]
        for s in range(4):
            slot = lax.rem(y + 4 - s, 4)
            q_ref[slot] = q_in[s][...]
            g_ref[slot] = q_in[4 + s][...]
    half_setup(meta_ref, rels, kv_in, k_ref, v_ref, kpos_ref, kspan_ref)

    def update(slot, ranges):
        parts, top = [], None
        for lo, hi, masked in ranges:
            scores = dot_nt(q_ref[slot], k_ref[lo:hi, :])
            if masked:
                scores = jnp.where(visible(meta_ref, slot, slice(lo, hi), kpos_ref, kspan_ref), scores, NEG)
            for c in range(0, hi - lo, HD):
                piece = scores[:, c : c + HD]
                top = piece if top is None else jnp.maximum(top, piece)
            parts.append(scores)
        new = jnp.broadcast_to(jnp.max(top, axis=1, keepdims=True) * SCALE2, (TOK, HD))
        mass, out = None, None
        if far:
            old = m_ref[slot]
            new = jnp.maximum(old, new)
            fade = jnp.exp2(old - new)
            mass, out = l_ref[slot] * fade, o_ref[slot] * fade
        m_ref[slot] = new
        for (lo, hi, masked), scores in zip(ranges, parts):
            weights = jnp.exp2(scores * SCALE2 - lanes(new, hi - lo))
            for c in range(0, hi - lo, HD):
                piece = weights[:, c : c + HD]
                mass = piece if mass is None else mass + piece
            term = dot_nn(weights.astype(BF), v_ref[lo:hi, :])
            out = term if out is None else out + term
        l_ref[slot] = mass
        o_ref[slot] = out

    each_slot(meta_ref, rels, update)

    if far:
        for s in range(4):
            slot = lax.rem(y + 4 - s, 4)
            mass = jnp.sum(l_ref[slot], axis=1, keepdims=True)
            attended = (o_ref[slot] * (1.0 / mass)).astype(BF)
            att_out[s][...] = attended
            lse_ref[slot] = m_ref[slot] + jnp.log2(mass)
            delta = jnp.sum(g_ref[slot].astype(F32) * attended.astype(F32), axis=1, keepdims=True)
            delta_ref[slot] = jnp.broadcast_to(delta, (TOK, HD))


WIDE = jax.ShapeDtypeStruct((4, TOK, HD), F32)
TALL = jax.ShapeDtypeStruct((4, TOK, HD), BF)
NARROW = jax.ShapeDtypeStruct((TOK, HD), BF)


def half_scratch():
    return [
        pltpu.VMEM((4 * HALF, HD), BF),
        pltpu.VMEM((4 * HALF, HD), BF),
        pltpu.VMEM((8, 4 * HALF), jnp.int32),
        pltpu.VMEM((8, 4 * HALF), jnp.int32),
    ]


def cost(dots):
    flops = dots * 10 * 2 * TOK * HALF * HD
    return pl.CostEstimate(flops=flops, bytes_accessed=8 * MIB, transcendentals=10 * TOK * HALF)


def forward(rels, meta, q, kv):
    far = 3 in rels
    out_shape = [NARROW] * 4 + [WIDE] * 2 if far else [TALL] * 2 + [WIDE] * 3
    return pl.pallas_call(
        functools.partial(forward_kernel, rels),
        out_shape=out_shape,
        in_specs=[smem()] + [vmem()] * (len(q) + 4),
        out_specs=[vmem()] * len(out_shape),
        scratch_shapes=([pltpu.VMEM((4, TOK, HD), F32)] * 3 if far else []) + half_scratch(),
        compiler_params=pltpu.CompilerParams(vmem_limit_bytes=32 * MIB),
        cost_estimate=cost(2),
        name="forward_far" if far else "forward_near",
    )(meta, *q, *kv)


def backward_kernel(rels, meta_ref, q_ref, g_ref, lse_ref, delta_ref, *rest):
    far = 3 in rels
    if not far:
        dq_in, rest = rest[0], rest[1:]
    kv_in, rest = rest[:4], rest[4:]
    dq_out, (keep_ref, send_ref) = rest[: 1 if far else 4], rest[-11:-9]
    k_ref, v_ref, kpos_ref, kspan_ref, qt_ref, gt_ref, dk_ref, dv_ref, dq_ref = rest[-9:]
    y = meta_ref[0]
    dq_ref[...] = jnp.zeros_like(dq_ref) if far else dq_in[...]
    for slot in range(4):
        qt_ref[slot] = q_ref[slot].T
        gt_ref[slot] = g_ref[slot].T

    def update(slot, ranges):
        q, g = q_ref[slot], g_ref[slot]
        dq = dq_ref[slot]
        for lo, hi, masked in ranges:
            k, v = k_ref[lo:hi, :], v_ref[lo:hi, :]
            probs = jnp.exp2(dot_nt(q, k) * SCALE2 - lanes(lse_ref[slot], hi - lo))
            if masked:
                probs = jnp.where(visible(meta_ref, slot, slice(lo, hi), kpos_ref, kspan_ref), probs, 0.0)
            score_grad = (probs * (dot_nt(g, v) - lanes(delta_ref[slot], hi - lo))).astype(BF)
            dq = dq + dot_nn(score_grad, k)
            dk_ref[:, lo:hi] += dot_nn(qt_ref[slot], score_grad)
            dv_ref[:, lo:hi] += dot_nn(gt_ref[slot], probs.astype(BF))
        dq_ref[slot] = dq

    half_setup(meta_ref, rels, kv_in, k_ref, v_ref, kpos_ref, kspan_ref)
    dk_ref[...] = jnp.zeros_like(dk_ref)
    dv_ref[...] = jnp.zeros_like(dv_ref)
    each_slot(meta_ref, rels, update)
    for i, s in enumerate(ORDER):
        group = lax.rem(y + 4 - s, 4)
        of = pl.ds(pl.multiple_of(group * HALF, HD), HALF)
        key_grad = (dk_ref[:, of] * SCALE).T.astype(BF)
        value_grad = dv_ref[:, of].T.astype(BF)
        at = slice(i * TOK, (i + 1) * TOK)
        keep_ref[at, :HD] = key_grad[:TOK]
        keep_ref[at, HD:] = value_grad[:TOK]
        send_ref[at, :HD] = key_grad[TOK:]
        send_ref[at, HD:] = value_grad[TOK:]
    if far:
        dq_out[0][...] = dq_ref[...]
    else:
        for s in range(4):
            dq_out[s][...] = (dq_ref[lax.rem(y + 4 - s, 4)] * SCALE).astype(BF)


def backward(rels, meta, stats, dq, kv):
    far = 3 in rels
    dq_shape = [WIDE] if far else [NARROW] * 4
    out = pl.pallas_call(
        functools.partial(backward_kernel, rels),
        out_shape=dq_shape + [jax.ShapeDtypeStruct((4 * TOK, 2 * HD), BF)] * 2,
        in_specs=[smem()] + [vmem()] * (4 + len(dq) + 4),
        out_specs=[vmem()] * (len(dq_shape) + 2),
        scratch_shapes=half_scratch()
        + [
            pltpu.VMEM((4, HD, TOK), BF),
            pltpu.VMEM((4, HD, TOK), BF),
            pltpu.VMEM((HD, 4 * HALF), F32),
            pltpu.VMEM((HD, 4 * HALF), F32),
            pltpu.VMEM((4, TOK, HD), F32),
        ],
        compiler_params=pltpu.CompilerParams(vmem_limit_bytes=32 * MIB),
        cost_estimate=cost(5),
        name="backward_far" if far else "backward_near",
    )(meta, *stats, *dq, *kv)
    return out[: len(dq_shape)], out[-2], out[-1]


def merge_kernel(rows, with_att, near_ref, recv_ref, far_ref, *rest):
    n = len(rows)
    dq, att, outs = rest[:n], rest[n : 2 * n] if with_att else (), rest[-n:]
    for i, row in enumerate(rows):
        at = slice(row * TOK, (row + 1) * TOK)
        total = near_ref[at, :].astype(F32) + recv_ref[at, :].astype(F32)
        total = total + far_ref[i * TOK : (i + 1) * TOK, :].astype(F32)
        outs[i][:, :HD] = dq[i][...]
        outs[i][:, HD : 3 * HD] = total.astype(BF)
        if with_att:
            outs[i][:, 3 * HD :] = att[i][...]


def merge(rows, near, recv, far, dq, att):
    width = 4 * HD if att else 3 * HD
    return pl.pallas_call(
        functools.partial(merge_kernel, rows, bool(att)),
        out_shape=[jax.ShapeDtypeStruct((TOK, width), BF)] * len(rows),
        in_specs=[vmem()] * (3 + len(dq) + len(att)),
        out_specs=[vmem()] * len(rows),
        compiler_params=pltpu.CompilerParams(vmem_limit_bytes=12 * MIB),
        name="merge",
    )(near, recv, far, *dq, *att)


def project_kernel(meta_ref, wqk_ref, wv_ref, *rest):
    pieces, (parts_ref, wide_ref, cut_ref) = rest[0:4], rest[4:]
    y = meta_ref[0]
    total = jnp.zeros((IMG, wqk_ref.shape[0]), F32)
    for s in range(4):
        head = lax.rem(y + 4 - s, 4)
        at = [pl.ds(pl.multiple_of((4 * i + head) * HD, HD), HD) for i in range(2)]
        w = jnp.concatenate([wqk_ref[:, at[0]], wqk_ref[:, at[1]], wv_ref[:, at[0]]], axis=1)
        total = total + dot_nt(pieces[s][TXT:, : 3 * HD], w)
    wide_ref[...] = jnp.zeros_like(wide_ref)
    wide_ref[:, 8:72, :] = total.reshape(4, 64, total.shape[1])
    for c in range(8):
        for i in range(4):
            cut_ref[10 * i : 10 * i + 10, :] = wide_ref[i, 8 * c + 7 : 8 * c + 17, :]
        parts_ref[c] = cut_ref[...].astype(BF)


def project(meta, w_qk, w_v, pieces):
    channels = w_qk.shape[0]
    return pl.pallas_call(
        project_kernel,
        out_shape=jax.ShapeDtypeStruct((8, 40, channels), BF),
        in_specs=[smem()] + [vmem()] * 6,
        out_specs=vmem(),
        scratch_shapes=[pltpu.VMEM((4, 80, channels), F32), pltpu.VMEM((40, channels), F32)],
        compiler_params=pltpu.CompilerParams(vmem_limit_bytes=16 * MIB),
        name="project",
    )(meta, w_qk, w_v, *pieces)


def unfold_kernel(meta_ref, *rest):
    pieces, att, (text_ref, att_ref, order_ref) = rest[0:4], rest[4:6], rest[6:]
    y = meta_ref[0]
    place, _ = row_places(meta_ref, 4 * y + meta_ref[1], lax.broadcasted_iota(jnp.int32, (TOK, TOK), 1))
    order_ref[...] = (place == lax.broadcasted_iota(jnp.int32, (TOK, TOK), 0)).astype(BF)
    for s in range(4):
        at = pl.ds(pl.multiple_of(lax.rem(y + 4 - s, 4) * HD, HD), HD)
        for i in range(3):
            text_ref[i, :, at] = pieces[s][:TXT, i * HD : (i + 1) * HD]
        rows = att[s // 2][...] if s % 2 == 0 else pieces[s][:, 3 * HD :]
        att_ref[:, at] = dot_nn(order_ref[...], rows).astype(BF)


def unfold(meta, pieces, att):
    return pl.pallas_call(
        unfold_kernel,
        out_shape=[jax.ShapeDtypeStruct((3, TXT, 4 * HD), BF), jax.ShapeDtypeStruct((TOK, 4 * HD), BF)],
        in_specs=[smem()] + [vmem()] * 6,
        out_specs=[vmem()] * 2,
        scratch_shapes=[pltpu.VMEM((TOK, TOK), BF)],
        compiler_params=pltpu.CompilerParams(vmem_limit_bytes=8 * MIB),
        cost_estimate=pl.CostEstimate(flops=8 * TOK * TOK * HD, bytes_accessed=4 * MIB, transcendentals=0),
        name="unfold",
    )(meta, *pieces, *att)


def slope_kernel(above_ref, eg_ref, below_ref, features_ref, conv_ref, out_ref, wide_ref):
    wide_ref[0, :10] = above_ref[...].astype(F32)
    for i in range(4):
        wide_ref[i + 1, :10] = eg_ref[...].astype(F32)[10 * i : 10 * i + 10]
    wide_ref[5, :10] = below_ref[...].astype(F32)
    value = features_ref[...].astype(F32)
    sigma = 1.0 / (1.0 + jnp.exp(-value))
    slope = sigma * (1.0 + value * (1.0 - sigma))
    total = jnp.zeros(out_ref.shape, F32)
    for a in range(3):
        for b in range(3):
            window = wide_ref[2 - a : 6 - a, 2 - b : 10 - b, :].reshape(out_ref.shape).astype(BF)
            total = total + dot_nt(window, conv_ref[a, b])
    center = wide_ref[1:5, 1:9, :].reshape(out_ref.shape)
    out_ref[...] = (center + slope * total).astype(BF)


def slope(above, eg, below, features, conv_weight):
    channels = features.shape[1]
    return pl.pallas_call(
        slope_kernel,
        out_shape=jax.ShapeDtypeStruct(features.shape, BF),
        in_specs=[vmem()] * 5,
        out_specs=vmem(),
        scratch_shapes=[pltpu.VMEM((6, 16, channels), F32)],
        compiler_params=pltpu.CompilerParams(vmem_limit_bytes=12 * MIB),
        name="slope",
    )(above, eg, below, features, conv_weight)


def local(features, conv_weight, w_query_key, w_value, text_qkv, span_ids, out_cot):
    seq = lax.axis_index("seq")
    y, j = seq // 4, seq % 4
    rows, columns, channels = features.shape
    up = [(i, i + 1) for i in range(15)]
    down = [(i + 1, i) for i in range(15)]
    shift_y = [[(i, (i + 4 * s) % 16) for i in range(16)] for s in range(4)]
    swap_core = [(i, i ^ 1) for i in range(16)]
    swap_x = [(i, i ^ 2) for i in range(16)]

    copies = jnp.broadcast_to(features[None], (8,) + features.shape)
    band = lax.all_to_all(copies, "col", 0, 0, tiled=True)
    above = lax.ppermute(band[:, rows - 1], "seq", up)
    below = lax.ppermute(band[:, 0], "seq", down)

    spans = span_ids.reshape(16, TOK)
    offsets = jnp.arange(TOK, dtype=jnp.int32)
    first = jnp.min(jnp.where(spans >= 0, offsets[None, :], TOK), axis=1)
    span = jnp.max(spans, axis=1)
    ends, starts = spans[3:15:4, -1], spans[4:16:4, 0]
    joined = (ends >= 0) & (ends == starts) & (j == 3)
    scalars = [jnp.stack([y, j]), joined, jnp.zeros((3,), jnp.int32), first, span]
    meta = jnp.concatenate([part.astype(jnp.int32) for part in scalars])

    w_qk = w_query_key.reshape(channels, 8 * HD)
    taps = stage(conv_weight, "stage")
    g = turn(meta, jnp.transpose(out_cot.reshape(TOK, 4, HD), (1, 0, 2)))
    g = [lax.ppermute(g[s], "seq", shift_y[s]) if s else g[0] for s in range(4)]
    acc = inner(band, taps)
    above, below, acc, g = lax.optimization_barrier((above, below, acc, g))
    out = encode(meta, acc, above, below, taps, w_qk, w_value, text_qkv.reshape(TXT, 12 * HD))
    q = list(out[4:])
    own = [out[0], jnp.concatenate([lax.ppermute(out[s], "seq", shift_y[s]) for s in ORDER[:3]])]
    crossed = [lax.ppermute(own[0], "seq", swap_x)]
    q[1], q[2], q[3], own[1], crossed[0] = lax.optimization_barrier((q[1], q[2], q[3], own[1], crossed[0]))
    q = [lax.ppermute(q[s], "seq", shift_y[s]) if s else q[0] for s in range(4)]
    crossed.append(lax.ppermute(own[1], "seq", swap_x))
    near_kv = own + [lax.ppermute(piece, "seq", swap_core) for piece in own]
    q, g, *state = forward((0, 1), meta, q + g, near_kv)
    crossed, state = lax.optimization_barrier((crossed, state))
    far_kv = crossed + [lax.ppermute(piece, "seq", swap_core) for piece in crossed]
    *att, lse, delta = forward((2, 3), meta, [q, g, *state], far_kv)
    stats = [q, g, lse, delta]

    def back(piece, s):
        return lax.ppermute(piece, "seq", shift_y[4 - s])

    dq, keep, send = backward((2, 3), meta, stats, [], far_kv)
    far = (keep.astype(F32) + lax.ppermute(send, "seq", swap_core).astype(F32)).astype(BF)
    far, dq = lax.optimization_barrier((far, dq))
    far = [lax.ppermute(far[a * TOK : (a + 2) * TOK], "seq", swap_x) for a in (0, 2)]
    dq, keep, send = backward((0, 1), meta, stats, dq, near_kv)
    att2 = back(att[2], 2)
    far[0], dq, keep, send, att2 = lax.optimization_barrier((far[0], dq, keep, send, att2))
    recv = lax.ppermute(send, "seq", swap_core)
    piece1, piece3 = merge((0, 1), keep, recv, far[0], [dq[1], dq[3]], [att[1], att[3]])
    piece1, piece3 = back(piece1, 1), back(piece3, 3)
    piece2, piece0 = merge((2, 3), keep, recv, far[1], [dq[2], dq[0]], [])
    piece2 = back(piece2, 2)
    pieces = [piece0, piece3, piece2, piece1]
    parts = project(meta, w_qk, w_value, pieces)
    parts, pieces = lax.optimization_barrier((parts, pieces))
    text_grad, attended = unfold(meta, pieces, [att[0], att2])
    text_grad = jnp.transpose(text_grad, (1, 0, 2))

    conv_weight, parts = lax.optimization_barrier((conv_weight, parts))
    taps = stage(conv_weight, "stage_again")
    parts = lax.all_to_all(parts, "col", 0, 0, tiled=True)
    parts, text_grad, attended = lax.optimization_barrier((parts, text_grad, attended))
    eg = jnp.sum(parts.astype(F32), axis=0).astype(BF)
    eg_above = lax.ppermute(eg[30:], "seq", up)
    eg_below = lax.ppermute(eg[:10], "seq", down)
    feature_grad = slope(eg_above, eg, eg_below, features.reshape(rows * columns, channels), taps)
    return (attended, feature_grad.reshape(features.shape), text_grad)


def solution(mesh):
    in_specs = (
        P("seq", "col", None),
        P(),
        P(None, None, "col"),
        P(None, "col"),
        P("seq", None, "col"),
        P(),
        P("seq", "col"),
    )
    out_specs = (P("seq", "col"), P("seq", "col", None), P("seq", None, "col"))
    return jax.shard_map(local, mesh=mesh, in_specs=in_specs, out_specs=out_specs, check_vma=False)
```

```python
import functools
import math

import jax
import jax.numpy as jnp
from jax import lax
from jax.experimental import pallas as pl
from jax.experimental.pallas import tpu as pltpu
from jax.sharding import PartitionSpec as P

HD = 128
TXT = 64
IMG = 256
TOK = 320
HALF = 2 * TOK
ORDER = (1, 3, 2, 0)
SCALE = HD ** -0.5
SCALE2 = SCALE * math.log2(math.e)
NEG = -1e30
BF = jnp.bfloat16
F32 = jnp.float32
MIB = 1024 * 1024


def dot_nt(a, b):
    return lax.dot_general(a, b, (((1,), (1,)), ((), ())), preferred_element_type=F32)


def dot_nn(a, b):
    return lax.dot_general(a, b, (((1,), (0,)), ((), ())), preferred_element_type=F32)


def vmem():
    return pl.BlockSpec(memory_space=pltpu.VMEM)


def smem():
    return pl.BlockSpec(memory_space=pltpu.SMEM)


def lanes(x, width):
    return jnp.concatenate([x] * (width // HD), axis=1)


def row_places(meta_ref, block, index):
    first = meta_ref[8 + block]
    text = jnp.where(index < first, index, index + IMG)
    place = jnp.where(index >= TXT, first + index - TXT, text)
    return place, index >= TXT


def turn_kernel(meta_ref, cot_ref, *g_refs):
    y = meta_ref[0]
    place, _ = row_places(meta_ref, 4 * y + meta_ref[1], lax.broadcasted_iota(jnp.int32, (TOK, TOK), 0))
    order = (place == lax.broadcasted_iota(jnp.int32, (TOK, TOK), 1)).astype(BF)
    for s in range(4):
        g_refs[s][...] = dot_nn(order, cot_ref[lax.rem(y + s, 4)]).astype(BF)


def turn(meta, cot):
    return pl.pallas_call(
        turn_kernel,
        out_shape=[jax.ShapeDtypeStruct((TOK, HD), BF)] * 4,
        in_specs=[smem(), vmem()],
        out_specs=[vmem()] * 4,
        compiler_params=pltpu.CompilerParams(vmem_limit_bytes=8 * MIB),
        name="turn",
    )(meta, cot)


def shifted_act(wide):
    cells = wide.shape[0]
    act = (wide / (1.0 + jnp.exp(-wide))).astype(BF).astype(F32)
    column = lax.broadcasted_iota(jnp.int32, act.shape, 0) % 64
    left = jnp.where(column == 0, 0.0, pltpu.roll(act, 1, 0)).astype(BF)
    right = jnp.where(column == 63, 0.0, pltpu.roll(act, cells - 1, 0)).astype(BF)
    return left, act.astype(BF), right


def inner_kernel(band_ref, conv_ref, acc_ref, act_ref):
    for r in range(4):
        for c in range(8):
            at = r * 64 + c * 8
            acc_ref[at : at + 8, :] = band_ref[c, r].astype(F32)
    wide = acc_ref[...]
    for b, act in enumerate(shifted_act(wide)):
        act_ref[b] = act
    cells = wide.shape[0]
    total = wide
    for b in range(3):
        total = total + dot_nn(act_ref[b], conv_ref[1, b])
    acc_ref[...] = total
    low = acc_ref[64:, :]
    for b in range(3):
        low = low + dot_nn(act_ref[b, : cells - 64, :], conv_ref[0, b])
    acc_ref[64:, :] = low
    high = acc_ref[: cells - 64, :]
    for b in range(3):
        high = high + dot_nn(act_ref[b, 64:, :], conv_ref[2, b])
    acc_ref[: cells - 64, :] = high


def inner(band, conv_weight):
    channels = band.shape[3]
    return pl.pallas_call(
        inner_kernel,
        out_shape=jax.ShapeDtypeStruct((IMG, channels), F32),
        in_specs=[vmem()] * 2,
        out_specs=vmem(),
        scratch_shapes=[pltpu.VMEM((3, IMG, channels), BF)],
        compiler_params=pltpu.CompilerParams(vmem_limit_bytes=16 * MIB),
        name="inner",
    )(band, conv_weight)


def encode_kernel(meta_ref, acc_ref, above_ref, below_ref, conv_ref, wqk_ref, wv_ref, text_ref, *rest):
    kv_refs, q_refs = rest[:4], rest[4:8]
    edge_ref, encoded_ref = rest[8:]
    y = meta_ref[0]
    cells = acc_ref.shape[0]
    encoded_ref[...] = acc_ref[...].astype(BF)
    for rows_ref, a, at in ((above_ref, 0, 0), (below_ref, 2, cells - 64)):
        for c in range(8):
            edge_ref[8 * c : 8 * c + 8, :] = rows_ref[c].astype(F32)
        total = acc_ref[at : at + 64, :]
        for b, act in enumerate(shifted_act(edge_ref[...])):
            total = total + dot_nn(act, conv_ref[a, b])
        encoded_ref[at : at + 64, :] = total.astype(BF)
    encoded = encoded_ref[...]
    for s in range(4):
        head = lax.rem(y + s, 4)
        at = [pl.ds(pl.multiple_of((4 * i + head) * HD, HD), HD) for i in range(3)]
        w = jnp.concatenate([wqk_ref[:, at[0]], wqk_ref[:, at[1]], wv_ref[:, at[0]]], axis=1)
        qkv = dot_nn(encoded, w).astype(BF)
        q_refs[s][:TXT, :] = text_ref[:, at[0]]
        q_refs[s][TXT:, :] = qkv[:, :HD]
        kv_refs[s][:TXT, :HD] = text_ref[:, at[1]]
        kv_refs[s][:TXT, HD:] = text_ref[:, at[2]]
        kv_refs[s][TXT:, :] = qkv[:, HD:]


def encode(meta, acc, above, below, conv_weight, w_qk, w_v, text):
    channels = acc.shape[1]
    return pl.pallas_call(
        encode_kernel,
        out_shape=[jax.ShapeDtypeStruct((TOK, 2 * HD), BF)] * 4 + [jax.ShapeDtypeStruct((TOK, HD), BF)] * 4,
        in_specs=[smem()] + [vmem()] * 7,
        out_specs=[vmem()] * 8,
        scratch_shapes=[pltpu.VMEM((64, channels), F32), pltpu.VMEM((IMG, channels), BF)],
        compiler_params=pltpu.CompilerParams(vmem_limit_bytes=16 * MIB),
        name="encode",
    )(meta, acc, above, below, conv_weight, w_qk, w_v, text)


def half_setup(meta_ref, rels, kv, k_ref, v_ref, kpos_ref, kspan_ref):
    y, j = meta_ref[0], meta_ref[1]
    for s in range(4):
        group = lax.rem(y + 4 - s, 4)
        for i in range(2):
            at = pl.ds(pl.multiple_of(group * HALF + i * TOK, 64), TOK)
            piece, first = (kv[2 * i + 1], ORDER.index(s) * TOK) if s else (kv[2 * i], 0)
            k_ref[at, :] = piece[first : first + TOK, :HD]
            v_ref[at, :] = piece[first : first + TOK, HD:]
    for group in range(4):
        for i, rel in enumerate(rels):
            at = slice(group * HALF + i * TOK, group * HALF + (i + 1) * TOK)
            block = 4 * group + (j ^ rel)
            place, image = row_places(meta_ref, block, lax.broadcasted_iota(jnp.int32, (8, TOK), 1))
            kpos_ref[:, at] = place + TOK * block
            kspan_ref[:, at] = jnp.where(image, meta_ref[24 + block], -1)


def visible(meta_ref, slot, at, kpos_ref, kspan_ref):
    block = 4 * slot + meta_ref[1]
    place, image = row_places(meta_ref, block, lax.broadcasted_iota(jnp.int32, (TOK, HALF), 0))
    span = jnp.where(image, meta_ref[24 + block], -2)
    return (kpos_ref[:1, at] <= place + TOK * block) | (kspan_ref[:1, at] == span)


def each_slot(meta_ref, rels, update):
    for slot in range(1, 4):
        update(slot, pl.ds(0, slot * HALF), False)
    parts = 2 if 3 in rels else 1

    def partly(i, unused):
        slot, part = lax.div(i, parts), lax.rem(i, parts)

        @pl.when((part == 0) | (meta_ref[2 + slot] > 0))
        def _():
            update(slot, pl.ds(pl.multiple_of((slot + part) * HALF, HALF), HALF), True)

        return unused

    lax.fori_loop(0, 3 * parts + 1, partly, 0)


def forward_kernel(rels, meta_ref, *rest):
    far = 3 in rels
    n_in = 5 if far else 8
    q_in, kv_in, rest = rest[:n_in], rest[n_in : n_in + 4], rest[n_in + 4 :]
    k_ref, v_ref, kpos_ref, kspan_ref = rest[-4:]
    y = meta_ref[0]
    if far:
        q_ref, g_ref = q_in[:2]
        att_out, (lse_ref, delta_ref), (m_ref, l_ref, o_ref) = rest[:4], rest[4:6], rest[6:9]
        for mine, given in zip((m_ref, l_ref, o_ref), q_in[2:]):
            mine[...] = given[...]
    else:
        q_ref, g_ref, m_ref, l_ref, o_ref = rest[:5]
        for s in range(4):
            slot = lax.rem(y + 4 - s, 4)
            q_ref[slot] = q_in[s][...]
            g_ref[slot] = q_in[4 + s][...]
        m_ref[...] = jnp.full_like(m_ref, NEG)
        l_ref[...] = jnp.zeros_like(l_ref)
        o_ref[...] = jnp.zeros_like(o_ref)
    half_setup(meta_ref, rels, kv_in, k_ref, v_ref, kpos_ref, kspan_ref)

    def update(slot, ranges):
        parts, top = [], None
        for at, masked in ranges:
            scores = dot_nt(q_ref[slot], k_ref[at, :])
            if masked:
                scores = jnp.where(visible(meta_ref, slot, at, kpos_ref, kspan_ref), scores, NEG)
            for c in range(0, scores.shape[1], HD):
                piece = scores[:, c : c + HD]
                top = piece if top is None else jnp.maximum(top, piece)
            parts.append((at, scores))
        old = m_ref[slot]
        new = jnp.maximum(old, jnp.max(top, axis=1, keepdims=True) * SCALE2)
        m_ref[slot] = new
        fade = jnp.exp2(old - new)
        mass, out = l_ref[slot] * fade, o_ref[slot] * fade
        for at, scores in parts:
            weights = jnp.exp2(scores * SCALE2 - lanes(new, scores.shape[1]))
            for c in range(0, scores.shape[1], HD):
                mass = mass + weights[:, c : c + HD]
            out = out + dot_nn(weights.astype(BF), v_ref[at, :])
        l_ref[slot] = mass
        o_ref[slot] = out

    for slot in range(4):
        whole = [(pl.ds(0, slot * HALF), False)] if slot else []
        update(slot, whole + [(pl.ds(slot * HALF, HALF), True)])
    if far:

        def joined(slot, unused):
            @pl.when(meta_ref[2 + slot] > 0)
            def _():
                update(slot, [(pl.ds(pl.multiple_of((slot + 1) * HALF, HALF), HALF), True)])

            return unused

        lax.fori_loop(0, 3, joined, 0)

    if far:
        for s in range(4):
            slot = lax.rem(y + 4 - s, 4)
            mass = jnp.sum(l_ref[slot], axis=1, keepdims=True)
            attended = (o_ref[slot] * (1.0 / mass)).astype(BF)
            att_out[s][...] = attended
            lse_ref[slot] = m_ref[slot] + jnp.log2(mass)
            delta = jnp.sum(g_ref[slot].astype(F32) * attended.astype(F32), axis=1, keepdims=True)
            delta_ref[slot] = jnp.broadcast_to(delta, (TOK, HD))


WIDE = jax.ShapeDtypeStruct((4, TOK, HD), F32)
TALL = jax.ShapeDtypeStruct((4, TOK, HD), BF)
NARROW = jax.ShapeDtypeStruct((TOK, HD), BF)


def half_scratch():
    return [
        pltpu.VMEM((4 * HALF, HD), BF),
        pltpu.VMEM((4 * HALF, HD), BF),
        pltpu.VMEM((8, 4 * HALF), jnp.int32),
        pltpu.VMEM((8, 4 * HALF), jnp.int32),
    ]


def cost(dots):
    flops = dots * 10 * 2 * TOK * HALF * HD
    return pl.CostEstimate(flops=flops, bytes_accessed=8 * MIB, transcendentals=10 * TOK * HALF)


def forward(rels, meta, q, kv):
    far = 3 in rels
    out_shape = [NARROW] * 4 + [WIDE] * 2 if far else [TALL] * 2 + [WIDE] * 3
    return pl.pallas_call(
        functools.partial(forward_kernel, rels),
        out_shape=out_shape,
        in_specs=[smem()] + [vmem()] * (len(q) + 4),
        out_specs=[vmem()] * len(out_shape),
        scratch_shapes=([pltpu.VMEM((4, TOK, HD), F32)] * 3 if far else []) + half_scratch(),
        compiler_params=pltpu.CompilerParams(vmem_limit_bytes=32 * MIB),
        cost_estimate=cost(2),
        name="forward_far" if far else "forward_near",
    )(meta, *q, *kv)


def backward_kernel(rels, meta_ref, q_ref, g_ref, lse_ref, delta_ref, *rest):
    far = 3 in rels
    if not far:
        dq_in, rest = rest[0], rest[1:]
    kv_in, rest = rest[:4], rest[4:]
    dq_out, (keep_ref, send_ref) = rest[: 1 if far else 4], rest[-11:-9]
    k_ref, v_ref, kpos_ref, kspan_ref, qt_ref, gt_ref, dk_ref, dv_ref, dq_ref = rest[-9:]
    y = meta_ref[0]
    dq_ref[...] = jnp.zeros_like(dq_ref) if far else dq_in[...]
    for slot in range(4):
        qt_ref[slot] = q_ref[slot].T
        gt_ref[slot] = g_ref[slot].T

    def update(slot, at, masked):
        k, v = k_ref[at, :], v_ref[at, :]
        width = k.shape[0]
        probs = jnp.exp2(dot_nt(q_ref[slot], k) * SCALE2 - lanes(lse_ref[slot], width))
        if masked:
            probs = jnp.where(visible(meta_ref, slot, at, kpos_ref, kspan_ref), probs, 0.0)
        score_grad = (probs * (dot_nt(g_ref[slot], v) - lanes(delta_ref[slot], width))).astype(BF)
        dq_ref[slot] += dot_nn(score_grad, k)
        dk_ref[:, at] += dot_nn(qt_ref[slot], score_grad)
        dv_ref[:, at] += dot_nn(gt_ref[slot], probs.astype(BF))

    half_setup(meta_ref, rels, kv_in, k_ref, v_ref, kpos_ref, kspan_ref)
    dk_ref[...] = jnp.zeros_like(dk_ref)
    dv_ref[...] = jnp.zeros_like(dv_ref)
    each_slot(meta_ref, rels, update)
    for i, s in enumerate(ORDER):
        group = lax.rem(y + 4 - s, 4)
        of = pl.ds(pl.multiple_of(group * HALF, HD), HALF)
        key_grad = (dk_ref[:, of] * SCALE).T.astype(BF)
        value_grad = dv_ref[:, of].T.astype(BF)
        at = slice(i * TOK, (i + 1) * TOK)
        keep_ref[at, :HD] = key_grad[:TOK]
        keep_ref[at, HD:] = value_grad[:TOK]
        send_ref[at, :HD] = key_grad[TOK:]
        send_ref[at, HD:] = value_grad[TOK:]
    if far:
        dq_out[0][...] = dq_ref[...]
    else:
        for s in range(4):
            dq_out[s][...] = (dq_ref[lax.rem(y + 4 - s, 4)] * SCALE).astype(BF)


def backward(rels, meta, stats, dq, kv):
    far = 3 in rels
    dq_shape = [WIDE] if far else [NARROW] * 4
    out = pl.pallas_call(
        functools.partial(backward_kernel, rels),
        out_shape=dq_shape + [jax.ShapeDtypeStruct((4 * TOK, 2 * HD), BF)] * 2,
        in_specs=[smem()] + [vmem()] * (4 + len(dq) + 4),
        out_specs=[vmem()] * (len(dq_shape) + 2),
        scratch_shapes=half_scratch()
        + [
            pltpu.VMEM((4, HD, TOK), BF),
            pltpu.VMEM((4, HD, TOK), BF),
            pltpu.VMEM((HD, 4 * HALF), F32),
            pltpu.VMEM((HD, 4 * HALF), F32),
            pltpu.VMEM((4, TOK, HD), F32),
        ],
        compiler_params=pltpu.CompilerParams(vmem_limit_bytes=32 * MIB),
        cost_estimate=cost(5),
        name="backward_far" if far else "backward_near",
    )(meta, *stats, *dq, *kv)
    return out[: len(dq_shape)], out[-2], out[-1]


def merge_kernel(rows, with_att, near_ref, recv_ref, far_ref, *rest):
    n = len(rows)
    dq, att, outs = rest[:n], rest[n : 2 * n] if with_att else (), rest[-n:]
    for i, row in enumerate(rows):
        at = slice(row * TOK, (row + 1) * TOK)
        total = near_ref[at, :].astype(F32) + recv_ref[at, :].astype(F32)
        total = total + far_ref[i * TOK : (i + 1) * TOK, :].astype(F32)
        outs[i][:, :HD] = dq[i][...]
        outs[i][:, HD : 3 * HD] = total.astype(BF)
        if with_att:
            outs[i][:, 3 * HD :] = att[i][...]


def merge(rows, near, recv, far, dq, att):
    width = 4 * HD if att else 3 * HD
    return pl.pallas_call(
        functools.partial(merge_kernel, rows, bool(att)),
        out_shape=[jax.ShapeDtypeStruct((TOK, width), BF)] * len(rows),
        in_specs=[vmem()] * (3 + len(dq) + len(att)),
        out_specs=[vmem()] * len(rows),
        compiler_params=pltpu.CompilerParams(vmem_limit_bytes=12 * MIB),
        name="merge",
    )(near, recv, far, *dq, *att)


def project_kernel(meta_ref, wqk_ref, wv_ref, *rest):
    pieces, (parts_ref, wide_ref, cut_ref) = rest[0:4], rest[4:]
    y = meta_ref[0]
    total = jnp.zeros((IMG, wqk_ref.shape[0]), F32)
    for s in range(4):
        head = lax.rem(y + 4 - s, 4)
        at = [pl.ds(pl.multiple_of((4 * i + head) * HD, HD), HD) for i in range(2)]
        w = jnp.concatenate([wqk_ref[:, at[0]], wqk_ref[:, at[1]], wv_ref[:, at[0]]], axis=1)
        total = total + dot_nt(pieces[s][TXT:, : 3 * HD], w)
    wide_ref[...] = jnp.zeros_like(wide_ref)
    wide_ref[:, 8:72, :] = total.reshape(4, 64, total.shape[1])
    for c in range(8):
        for i in range(4):
            cut_ref[10 * i : 10 * i + 10, :] = wide_ref[i, 8 * c + 7 : 8 * c + 17, :]
        parts_ref[c] = cut_ref[...].astype(BF)


def project(meta, w_qk, w_v, pieces):
    channels = w_qk.shape[0]
    return pl.pallas_call(
        project_kernel,
        out_shape=jax.ShapeDtypeStruct((8, 40, channels), BF),
        in_specs=[smem()] + [vmem()] * 6,
        out_specs=vmem(),
        scratch_shapes=[pltpu.VMEM((4, 80, channels), F32), pltpu.VMEM((40, channels), F32)],
        compiler_params=pltpu.CompilerParams(vmem_limit_bytes=16 * MIB),
        name="project",
    )(meta, w_qk, w_v, *pieces)


def unfold_kernel(meta_ref, *rest):
    pieces, att, (text_ref, att_ref, order_ref) = rest[0:4], rest[4:6], rest[6:]
    y = meta_ref[0]
    place, _ = row_places(meta_ref, 4 * y + meta_ref[1], lax.broadcasted_iota(jnp.int32, (TOK, TOK), 1))
    order_ref[...] = (place == lax.broadcasted_iota(jnp.int32, (TOK, TOK), 0)).astype(BF)
    for s in range(4):
        at = pl.ds(pl.multiple_of(lax.rem(y + 4 - s, 4) * HD, HD), HD)
        for i in range(3):
            text_ref[i, :, at] = pieces[s][:TXT, i * HD : (i + 1) * HD]
        rows = att[s // 2][...] if s % 2 == 0 else pieces[s][:, 3 * HD :]
        att_ref[:, at] = dot_nn(order_ref[...], rows).astype(BF)


def unfold(meta, pieces, att):
    return pl.pallas_call(
        unfold_kernel,
        out_shape=[jax.ShapeDtypeStruct((3, TXT, 4 * HD), BF), jax.ShapeDtypeStruct((TOK, 4 * HD), BF)],
        in_specs=[smem()] + [vmem()] * 6,
        out_specs=[vmem()] * 2,
        scratch_shapes=[pltpu.VMEM((TOK, TOK), BF)],
        compiler_params=pltpu.CompilerParams(vmem_limit_bytes=8 * MIB),
        cost_estimate=pl.CostEstimate(flops=8 * TOK * TOK * HD, bytes_accessed=4 * MIB, transcendentals=0),
        name="unfold",
    )(meta, *pieces, *att)


def slope_kernel(above_ref, eg_ref, below_ref, features_ref, conv_ref, out_ref, wide_ref):
    wide_ref[0, :10] = above_ref[...].astype(F32)
    for i in range(4):
        wide_ref[i + 1, :10] = eg_ref[...].astype(F32)[10 * i : 10 * i + 10]
    wide_ref[5, :10] = below_ref[...].astype(F32)
    value = features_ref[...].astype(F32)
    sigma = 1.0 / (1.0 + jnp.exp(-value))
    slope = sigma * (1.0 + value * (1.0 - sigma))
    total = jnp.zeros(out_ref.shape, F32)
    for a in range(3):
        for b in range(3):
            window = wide_ref[2 - a : 6 - a, 2 - b : 10 - b, :].reshape(out_ref.shape).astype(BF)
            total = total + dot_nt(window, conv_ref[a, b])
    center = wide_ref[1:5, 1:9, :].reshape(out_ref.shape)
    out_ref[...] = (center + slope * total).astype(BF)


def slope(above, eg, below, features, conv_weight):
    channels = features.shape[1]
    return pl.pallas_call(
        slope_kernel,
        out_shape=jax.ShapeDtypeStruct(features.shape, BF),
        in_specs=[vmem()] * 5,
        out_specs=vmem(),
        scratch_shapes=[pltpu.VMEM((6, 16, channels), F32)],
        compiler_params=pltpu.CompilerParams(vmem_limit_bytes=12 * MIB),
        name="slope",
    )(above, eg, below, features, conv_weight)


def local(features, conv_weight, w_query_key, w_value, text_qkv, span_ids, out_cot):
    seq = lax.axis_index("seq")
    y, j = seq // 4, seq % 4
    rows, columns, channels = features.shape
    up = [(i, i + 1) for i in range(15)]
    down = [(i + 1, i) for i in range(15)]
    shift_y = [[(i, (i + 4 * s) % 16) for i in range(16)] for s in range(4)]
    swap_core = [(i, i ^ 1) for i in range(16)]
    swap_x = [(i, i ^ 2) for i in range(16)]

    copies = jnp.broadcast_to(features[None], (8,) + features.shape)
    band = lax.all_to_all(copies, "col", 0, 0, tiled=True)
    above = lax.ppermute(band[:, rows - 1], "seq", up)
    below = lax.ppermute(band[:, 0], "seq", down)

    spans = span_ids.reshape(16, TOK)
    offsets = jnp.arange(TOK, dtype=jnp.int32)
    first = jnp.min(jnp.where(spans >= 0, offsets[None, :], TOK), axis=1)
    span = jnp.max(spans, axis=1)
    ends, starts = spans[3:15:4, -1], spans[4:16:4, 0]
    joined = (ends >= 0) & (ends == starts) & (j == 3)
    scalars = [jnp.stack([y, j]), joined, jnp.zeros((3,), jnp.int32), first, span]
    meta = jnp.concatenate([part.astype(jnp.int32) for part in scalars])

    w_qk = w_query_key.reshape(channels, 8 * HD)
    g = turn(meta, jnp.transpose(out_cot.reshape(TOK, 4, HD), (1, 0, 2)))
    g = [lax.ppermute(g[s], "seq", shift_y[s]) if s else g[0] for s in range(4)]
    acc = inner(band, conv_weight)
    above, below, acc, g = lax.optimization_barrier((above, below, acc, g))
    out = encode(meta, acc, above, below, conv_weight, w_qk, w_value, text_qkv.reshape(TXT, 12 * HD))
    q = list(out[4:])
    own = [out[0], jnp.concatenate([lax.ppermute(out[s], "seq", shift_y[s]) for s in ORDER[:3]])]
    crossed = [lax.ppermute(own[0], "seq", swap_x)]
    q[1], q[2], q[3], own[1], crossed[0] = lax.optimization_barrier((q[1], q[2], q[3], own[1], crossed[0]))
    q = [lax.ppermute(q[s], "seq", shift_y[s]) if s else q[0] for s in range(4)]
    crossed.append(lax.ppermute(own[1], "seq", swap_x))
    near_kv = own + [lax.ppermute(piece, "seq", swap_core) for piece in own]
    q, g, *state = forward((0, 1), meta, q + g, near_kv)
    crossed, state = lax.optimization_barrier((crossed, state))
    far_kv = crossed + [lax.ppermute(piece, "seq", swap_core) for piece in crossed]
    *att, lse, delta = forward((2, 3), meta, [q, g, *state], far_kv)
    stats = [q, g, lse, delta]

    def back(piece, s):
        return lax.ppermute(piece, "seq", shift_y[4 - s])

    dq, keep, send = backward((2, 3), meta, stats, [], far_kv)
    far = (keep.astype(F32) + lax.ppermute(send, "seq", swap_core).astype(F32)).astype(BF)
    far, dq = lax.optimization_barrier((far, dq))
    far = [lax.ppermute(far[a * TOK : (a + 2) * TOK], "seq", swap_x) for a in (0, 2)]
    dq, keep, send = backward((0, 1), meta, stats, dq, near_kv)
    att2 = back(att[2], 2)
    far[0], dq, keep, send, att2 = lax.optimization_barrier((far[0], dq, keep, send, att2))
    recv = lax.ppermute(send, "seq", swap_core)
    piece1, piece3 = merge((0, 1), keep, recv, far[0], [dq[1], dq[3]], [att[1], att[3]])
    piece1, piece3 = back(piece1, 1), back(piece3, 3)
    piece2, piece0 = merge((2, 3), keep, recv, far[1], [dq[2], dq[0]], [])
    piece2 = back(piece2, 2)
    pieces = [piece0, piece3, piece2, piece1]
    parts = project(meta, w_qk, w_value, pieces)
    parts, pieces = lax.optimization_barrier((parts, pieces))
    text_grad, attended = unfold(meta, pieces, [att[0], att2])
    text_grad = jnp.transpose(text_grad, (1, 0, 2))

    parts = lax.all_to_all(parts, "col", 0, 0, tiled=True)
    parts, text_grad, attended = lax.optimization_barrier((parts, text_grad, attended))
    eg = jnp.sum(parts.astype(F32), axis=0).astype(BF)
    eg_above = lax.ppermute(eg[30:], "seq", up)
    eg_below = lax.ppermute(eg[:10], "seq", down)
    feature_grad = slope(eg_above, eg, eg_below, features.reshape(rows * columns, channels), conv_weight)
    return (attended, feature_grad.reshape(features.shape), text_grad)


def solution(mesh):
    in_specs = (
        P("seq", "col", None),
        P(),
        P(None, None, "col"),
        P(None, "col"),
        P("seq", None, "col"),
        P(),
        P("seq", "col"),
    )
    out_specs = (P("seq", "col"), P("seq", "col", None), P("seq", None, "col"))
    return jax.shard_map(local, mesh=mesh, in_specs=in_specs, out_specs=out_specs, check_vma=False)
```

```python
import functools
import math

import jax
import jax.numpy as jnp
from jax import lax
from jax.experimental import pallas as pl
from jax.experimental.pallas import tpu as pltpu
from jax.sharding import PartitionSpec as P

HD = 128
TXT = 64
IMG = 256
TOK = 320
HALF = 2 * TOK
ORDER = (1, 3, 2, 0)
SCALE = HD ** -0.5
SCALE2 = SCALE * math.log2(math.e)
NEG = -1e30
BF = jnp.bfloat16
F32 = jnp.float32
MIB = 1024 * 1024


def dot_nt(a, b):
    return lax.dot_general(a, b, (((1,), (1,)), ((), ())), preferred_element_type=F32)


def dot_nn(a, b):
    return lax.dot_general(a, b, (((1,), (0,)), ((), ())), preferred_element_type=F32)


def vmem():
    return pl.BlockSpec(memory_space=pltpu.VMEM)


def smem():
    return pl.BlockSpec(memory_space=pltpu.SMEM)


def lanes(x, width):
    return jnp.concatenate([x] * (width // HD), axis=1)


def row_places(meta_ref, block, index):
    first = meta_ref[8 + block]
    text = jnp.where(index < first, index, index + IMG)
    place = jnp.where(index >= TXT, first + index - TXT, text)
    return place, index >= TXT


def turn_kernel(meta_ref, cot_ref, *g_refs):
    y = meta_ref[0]
    place, _ = row_places(meta_ref, 4 * y + meta_ref[1], lax.broadcasted_iota(jnp.int32, (TOK, TOK), 0))
    order = (place == lax.broadcasted_iota(jnp.int32, (TOK, TOK), 1)).astype(BF)
    for s in range(4):
        g_refs[s][...] = dot_nn(order, cot_ref[lax.rem(y + s, 4)]).astype(BF)


def turn(meta, cot):
    return pl.pallas_call(
        turn_kernel,
        out_shape=[jax.ShapeDtypeStruct((TOK, HD), BF)] * 4,
        in_specs=[smem(), vmem()],
        out_specs=[vmem()] * 4,
        compiler_params=pltpu.CompilerParams(vmem_limit_bytes=8 * MIB),
        name="turn",
    )(meta, cot)


def stage_kernel(in_ref, out_ref, sems):
    copies = [
        pltpu.make_async_copy(in_ref.at[i // 3, i % 3], out_ref.at[i // 3, i % 3], sems.at[i]) for i in range(9)
    ]
    for copy in copies:
        copy.start()
    for copy in copies:
        copy.wait()


def stage(conv_weight):
    return pl.pallas_call(
        stage_kernel,
        out_shape=jax.ShapeDtypeStruct(conv_weight.shape, BF),
        in_specs=[pl.BlockSpec(memory_space=pltpu.HBM)],
        out_specs=vmem(),
        scratch_shapes=[pltpu.SemaphoreType.DMA((9,))],
        compiler_params=pltpu.CompilerParams(vmem_limit_bytes=8 * MIB),
        name="stage",
    )(conv_weight)


def shifted_act(wide):
    cells = wide.shape[0]
    act = (wide / (1.0 + jnp.exp(-wide))).astype(BF).astype(F32)
    column = lax.broadcasted_iota(jnp.int32, act.shape, 0) % 64
    left = jnp.where(column == 0, 0.0, pltpu.roll(act, 1, 0)).astype(BF)
    right = jnp.where(column == 63, 0.0, pltpu.roll(act, cells - 1, 0)).astype(BF)
    return left, act.astype(BF), right


def inner_kernel(band_ref, conv_ref, acc_ref, act_ref):
    for r in range(4):
        for c in range(8):
            at = r * 64 + c * 8
            acc_ref[at : at + 8, :] = band_ref[c, r].astype(F32)
    wide = acc_ref[...]
    for b, act in enumerate(shifted_act(wide)):
        act_ref[b] = act
    cells = wide.shape[0]
    total = wide
    for b in range(3):
        total = total + dot_nn(act_ref[b], conv_ref[1, b])
    acc_ref[...] = total
    low = acc_ref[64:, :]
    for b in range(3):
        low = low + dot_nn(act_ref[b, : cells - 64, :], conv_ref[0, b])
    acc_ref[64:, :] = low
    high = acc_ref[: cells - 64, :]
    for b in range(3):
        high = high + dot_nn(act_ref[b, 64:, :], conv_ref[2, b])
    acc_ref[: cells - 64, :] = high


def inner(band, conv_weight):
    channels = band.shape[3]
    return pl.pallas_call(
        inner_kernel,
        out_shape=jax.ShapeDtypeStruct((IMG, channels), F32),
        in_specs=[vmem()] * 2,
        out_specs=vmem(),
        scratch_shapes=[pltpu.VMEM((3, IMG, channels), BF)],
        compiler_params=pltpu.CompilerParams(vmem_limit_bytes=16 * MIB),
        name="inner",
    )(band, conv_weight)


def encode_kernel(meta_ref, acc_ref, above_ref, below_ref, conv_ref, wqk_ref, wv_ref, text_ref, *rest):
    kv_refs, q_refs = rest[:4], rest[4:8]
    edge_ref, encoded_ref = rest[8:]
    y = meta_ref[0]
    cells = acc_ref.shape[0]
    encoded_ref[...] = acc_ref[...].astype(BF)
    for rows_ref, a, at in ((above_ref, 0, 0), (below_ref, 2, cells - 64)):
        for c in range(8):
            edge_ref[8 * c : 8 * c + 8, :] = rows_ref[c].astype(F32)
        total = acc_ref[at : at + 64, :]
        for b, act in enumerate(shifted_act(edge_ref[...])):
            total = total + dot_nn(act, conv_ref[a, b])
        encoded_ref[at : at + 64, :] = total.astype(BF)
    encoded = encoded_ref[...]
    for s in range(4):
        head = lax.rem(y + s, 4)
        at = [pl.ds(pl.multiple_of((4 * i + head) * HD, HD), HD) for i in range(3)]
        w = jnp.concatenate([wqk_ref[:, at[0]], wqk_ref[:, at[1]], wv_ref[:, at[0]]], axis=1)
        qkv = dot_nn(encoded, w).astype(BF)
        q_refs[s][:TXT, :] = text_ref[:, at[0]]
        q_refs[s][TXT:, :] = qkv[:, :HD]
        kv_refs[s][:TXT, :HD] = text_ref[:, at[1]]
        kv_refs[s][:TXT, HD:] = text_ref[:, at[2]]
        kv_refs[s][TXT:, :] = qkv[:, HD:]


def encode(meta, acc, above, below, conv_weight, w_qk, w_v, text):
    channels = acc.shape[1]
    return pl.pallas_call(
        encode_kernel,
        out_shape=[jax.ShapeDtypeStruct((TOK, 2 * HD), BF)] * 4 + [jax.ShapeDtypeStruct((TOK, HD), BF)] * 4,
        in_specs=[smem()] + [vmem()] * 7,
        out_specs=[vmem()] * 8,
        scratch_shapes=[pltpu.VMEM((64, channels), F32), pltpu.VMEM((IMG, channels), BF)],
        compiler_params=pltpu.CompilerParams(vmem_limit_bytes=16 * MIB),
        name="encode",
    )(meta, acc, above, below, conv_weight, w_qk, w_v, text)


def half_setup(meta_ref, rels, kv, k_ref, v_ref, kpos_ref, kspan_ref):
    y, j = meta_ref[0], meta_ref[1]
    for s in range(4):
        group = lax.rem(y + 4 - s, 4)
        for i in range(2):
            at = pl.ds(pl.multiple_of(group * HALF + i * TOK, 64), TOK)
            piece, first = (kv[2 * i + 1], ORDER.index(s) * TOK) if s else (kv[2 * i], 0)
            k_ref[at, :] = piece[first : first + TOK, :HD]
            v_ref[at, :] = piece[first : first + TOK, HD:]
    for group in range(4):
        for i, rel in enumerate(rels):
            at = slice(group * HALF + i * TOK, group * HALF + (i + 1) * TOK)
            block = 4 * group + (j ^ rel)
            place, image = row_places(meta_ref, block, lax.broadcasted_iota(jnp.int32, (8, TOK), 1))
            kpos_ref[:, at] = place + TOK * block
            kspan_ref[:, at] = jnp.where(image, meta_ref[24 + block], -1)


def visible(meta_ref, slot, at, kpos_ref, kspan_ref):
    block = 4 * slot + meta_ref[1]
    place, image = row_places(meta_ref, block, lax.broadcasted_iota(jnp.int32, (TOK, HALF), 0))
    span = jnp.where(image, meta_ref[24 + block], -2)
    return (kpos_ref[:1, at] <= place + TOK * block) | (kspan_ref[:1, at] == span)


def each_slot(meta_ref, rels, update):
    for slot in range(1, 4):
        update(slot, pl.ds(0, slot * HALF), False)
    parts = 2 if 3 in rels else 1

    def partly(i, unused):
        slot, part = lax.div(i, parts), lax.rem(i, parts)

        @pl.when((part == 0) | (meta_ref[2 + slot] > 0))
        def _():
            update(slot, pl.ds(pl.multiple_of((slot + part) * HALF, HALF), HALF), True)

        return unused

    lax.fori_loop(0, 3 * parts + 1, partly, 0)


def forward_kernel(rels, meta_ref, *rest):
    far = 3 in rels
    n_in = 5 if far else 8
    q_in, kv_in, rest = rest[:n_in], rest[n_in : n_in + 4], rest[n_in + 4 :]
    k_ref, v_ref, kpos_ref, kspan_ref = rest[-4:]
    y = meta_ref[0]
    if far:
        q_ref, g_ref = q_in[:2]
        att_out, (lse_ref, delta_ref), (m_ref, l_ref, o_ref) = rest[:4], rest[4:6], rest[6:9]
        for mine, given in zip((m_ref, l_ref, o_ref), q_in[2:]):
            mine[...] = given[...]
    else:
        q_ref, g_ref, m_ref, l_ref, o_ref = rest[:5]
        for s in range(4):
            slot = lax.rem(y + 4 - s, 4)
            q_ref[slot] = q_in[s][...]
            g_ref[slot] = q_in[4 + s][...]
        m_ref[...] = jnp.full_like(m_ref, NEG)
        l_ref[...] = jnp.zeros_like(l_ref)
        o_ref[...] = jnp.zeros_like(o_ref)
    half_setup(meta_ref, rels, kv_in, k_ref, v_ref, kpos_ref, kspan_ref)

    def update(slot, ranges):
        parts, top = [], None
        for at, masked in ranges:
            scores = dot_nt(q_ref[slot], k_ref[at, :])
            if masked:
                scores = jnp.where(visible(meta_ref, slot, at, kpos_ref, kspan_ref), scores, NEG)
            for c in range(0, scores.shape[1], HD):
                piece = scores[:, c : c + HD]
                top = piece if top is None else jnp.maximum(top, piece)
            parts.append((at, scores))
        old = m_ref[slot]
        new = jnp.maximum(old, jnp.max(top, axis=1, keepdims=True) * SCALE2)
        m_ref[slot] = new
        fade = jnp.exp2(old - new)
        mass, out = l_ref[slot] * fade, o_ref[slot] * fade
        for at, scores in parts:
            weights = jnp.exp2(scores * SCALE2 - lanes(new, scores.shape[1]))
            for c in range(0, scores.shape[1], HD):
                mass = mass + weights[:, c : c + HD]
            out = out + dot_nn(weights.astype(BF), v_ref[at, :])
        l_ref[slot] = mass
        o_ref[slot] = out

    for slot in range(4):
        whole = [(pl.ds(0, slot * HALF), False)] if slot else []
        update(slot, whole + [(pl.ds(slot * HALF, HALF), True)])
    if far:

        def joined(slot, unused):
            @pl.when(meta_ref[2 + slot] > 0)
            def _():
                update(slot, [(pl.ds(pl.multiple_of((slot + 1) * HALF, HALF), HALF), True)])

            return unused

        lax.fori_loop(0, 3, joined, 0)

    if far:
        for s in range(4):
            slot = lax.rem(y + 4 - s, 4)
            mass = jnp.sum(l_ref[slot], axis=1, keepdims=True)
            attended = (o_ref[slot] * (1.0 / mass)).astype(BF)
            att_out[s][...] = attended
            lse_ref[slot] = m_ref[slot] + jnp.log2(mass)
            delta = jnp.sum(g_ref[slot].astype(F32) * attended.astype(F32), axis=1, keepdims=True)
            delta_ref[slot] = jnp.broadcast_to(delta, (TOK, HD))


WIDE = jax.ShapeDtypeStruct((4, TOK, HD), F32)
TALL = jax.ShapeDtypeStruct((4, TOK, HD), BF)
NARROW = jax.ShapeDtypeStruct((TOK, HD), BF)


def half_scratch():
    return [
        pltpu.VMEM((4 * HALF, HD), BF),
        pltpu.VMEM((4 * HALF, HD), BF),
        pltpu.VMEM((8, 4 * HALF), jnp.int32),
        pltpu.VMEM((8, 4 * HALF), jnp.int32),
    ]


def cost(dots):
    flops = dots * 10 * 2 * TOK * HALF * HD
    return pl.CostEstimate(flops=flops, bytes_accessed=8 * MIB, transcendentals=10 * TOK * HALF)


def forward(rels, meta, q, kv):
    far = 3 in rels
    out_shape = [NARROW] * 4 + [WIDE] * 2 if far else [TALL] * 2 + [WIDE] * 3
    return pl.pallas_call(
        functools.partial(forward_kernel, rels),
        out_shape=out_shape,
        in_specs=[smem()] + [vmem()] * (len(q) + 4),
        out_specs=[vmem()] * len(out_shape),
        scratch_shapes=([pltpu.VMEM((4, TOK, HD), F32)] * 3 if far else []) + half_scratch(),
        compiler_params=pltpu.CompilerParams(vmem_limit_bytes=32 * MIB),
        cost_estimate=cost(2),
        name="forward_far" if far else "forward_near",
    )(meta, *q, *kv)


def backward_kernel(rels, meta_ref, q_ref, g_ref, lse_ref, delta_ref, *rest):
    far = 3 in rels
    if not far:
        dq_in, rest = rest[0], rest[1:]
    kv_in, rest = rest[:4], rest[4:]
    dq_out, (keep_ref, send_ref) = rest[: 1 if far else 4], rest[-11:-9]
    k_ref, v_ref, kpos_ref, kspan_ref, qt_ref, gt_ref, dk_ref, dv_ref, dq_ref = rest[-9:]
    y = meta_ref[0]
    dq_ref[...] = jnp.zeros_like(dq_ref) if far else dq_in[...]
    for slot in range(4):
        qt_ref[slot] = q_ref[slot].T
        gt_ref[slot] = g_ref[slot].T

    def update(slot, at, masked):
        k, v = k_ref[at, :], v_ref[at, :]
        width = k.shape[0]
        probs = jnp.exp2(dot_nt(q_ref[slot], k) * SCALE2 - lanes(lse_ref[slot], width))
        if masked:
            probs = jnp.where(visible(meta_ref, slot, at, kpos_ref, kspan_ref), probs, 0.0)
        score_grad = (probs * (dot_nt(g_ref[slot], v) - lanes(delta_ref[slot], width))).astype(BF)
        dq_ref[slot] += dot_nn(score_grad, k)
        dk_ref[:, at] += dot_nn(qt_ref[slot], score_grad)
        dv_ref[:, at] += dot_nn(gt_ref[slot], probs.astype(BF))

    half_setup(meta_ref, rels, kv_in, k_ref, v_ref, kpos_ref, kspan_ref)
    dk_ref[...] = jnp.zeros_like(dk_ref)
    dv_ref[...] = jnp.zeros_like(dv_ref)
    each_slot(meta_ref, rels, update)
    for i, s in enumerate(ORDER):
        group = lax.rem(y + 4 - s, 4)
        of = pl.ds(pl.multiple_of(group * HALF, HD), HALF)
        key_grad = (dk_ref[:, of] * SCALE).T.astype(BF)
        value_grad = dv_ref[:, of].T.astype(BF)
        at = slice(i * TOK, (i + 1) * TOK)
        keep_ref[at, :HD] = key_grad[:TOK]
        keep_ref[at, HD:] = value_grad[:TOK]
        send_ref[at, :HD] = key_grad[TOK:]
        send_ref[at, HD:] = value_grad[TOK:]
    if far:
        dq_out[0][...] = dq_ref[...]
    else:
        for s in range(4):
            dq_out[s][...] = (dq_ref[lax.rem(y + 4 - s, 4)] * SCALE).astype(BF)


def backward(rels, meta, stats, dq, kv):
    far = 3 in rels
    dq_shape = [WIDE] if far else [NARROW] * 4
    out = pl.pallas_call(
        functools.partial(backward_kernel, rels),
        out_shape=dq_shape + [jax.ShapeDtypeStruct((4 * TOK, 2 * HD), BF)] * 2,
        in_specs=[smem()] + [vmem()] * (4 + len(dq) + 4),
        out_specs=[vmem()] * (len(dq_shape) + 2),
        scratch_shapes=half_scratch()
        + [
            pltpu.VMEM((4, HD, TOK), BF),
            pltpu.VMEM((4, HD, TOK), BF),
            pltpu.VMEM((HD, 4 * HALF), F32),
            pltpu.VMEM((HD, 4 * HALF), F32),
            pltpu.VMEM((4, TOK, HD), F32),
        ],
        compiler_params=pltpu.CompilerParams(vmem_limit_bytes=32 * MIB),
        cost_estimate=cost(5),
        name="backward_far" if far else "backward_near",
    )(meta, *stats, *dq, *kv)
    return out[: len(dq_shape)], out[-2], out[-1]


def merge_kernel(rows, with_att, near_ref, recv_ref, far_ref, *rest):
    n = len(rows)
    dq, att, outs = rest[:n], rest[n : 2 * n] if with_att else (), rest[-n:]
    for i, row in enumerate(rows):
        at = slice(row * TOK, (row + 1) * TOK)
        total = near_ref[at, :].astype(F32) + recv_ref[at, :].astype(F32)
        total = total + far_ref[i * TOK : (i + 1) * TOK, :].astype(F32)
        outs[i][:, :HD] = dq[i][...]
        outs[i][:, HD : 3 * HD] = total.astype(BF)
        if with_att:
            outs[i][:, 3 * HD :] = att[i][...]


def merge(rows, near, recv, far, dq, att):
    width = 4 * HD if att else 3 * HD
    return pl.pallas_call(
        functools.partial(merge_kernel, rows, bool(att)),
        out_shape=[jax.ShapeDtypeStruct((TOK, width), BF)] * len(rows),
        in_specs=[vmem()] * (3 + len(dq) + len(att)),
        out_specs=[vmem()] * len(rows),
        compiler_params=pltpu.CompilerParams(vmem_limit_bytes=12 * MIB),
        name="merge",
    )(near, recv, far, *dq, *att)


def project_kernel(meta_ref, wqk_ref, wv_ref, *rest):
    pieces, (parts_ref, wide_ref, cut_ref) = rest[0:4], rest[4:]
    y = meta_ref[0]
    total = jnp.zeros((IMG, wqk_ref.shape[0]), F32)
    for s in range(4):
        head = lax.rem(y + 4 - s, 4)
        at = [pl.ds(pl.multiple_of((4 * i + head) * HD, HD), HD) for i in range(2)]
        w = jnp.concatenate([wqk_ref[:, at[0]], wqk_ref[:, at[1]], wv_ref[:, at[0]]], axis=1)
        total = total + dot_nt(pieces[s][TXT:, : 3 * HD], w)
    wide_ref[...] = jnp.zeros_like(wide_ref)
    wide_ref[:, 8:72, :] = total.reshape(4, 64, total.shape[1])
    for c in range(8):
        for i in range(4):
            cut_ref[10 * i : 10 * i + 10, :] = wide_ref[i, 8 * c + 7 : 8 * c + 17, :]
        parts_ref[c] = cut_ref[...].astype(BF)


def project(meta, w_qk, w_v, pieces):
    channels = w_qk.shape[0]
    return pl.pallas_call(
        project_kernel,
        out_shape=jax.ShapeDtypeStruct((8, 40, channels), BF),
        in_specs=[smem()] + [vmem()] * 6,
        out_specs=vmem(),
        scratch_shapes=[pltpu.VMEM((4, 80, channels), F32), pltpu.VMEM((40, channels), F32)],
        compiler_params=pltpu.CompilerParams(vmem_limit_bytes=16 * MIB),
        name="project",
    )(meta, w_qk, w_v, *pieces)


def unfold_kernel(meta_ref, *rest):
    pieces, att, (text_ref, att_ref, order_ref) = rest[0:4], rest[4:6], rest[6:]
    y = meta_ref[0]
    place, _ = row_places(meta_ref, 4 * y + meta_ref[1], lax.broadcasted_iota(jnp.int32, (TOK, TOK), 1))
    order_ref[...] = (place == lax.broadcasted_iota(jnp.int32, (TOK, TOK), 0)).astype(BF)
    for s in range(4):
        at = pl.ds(pl.multiple_of(lax.rem(y + 4 - s, 4) * HD, HD), HD)
        for i in range(3):
            text_ref[i, :, at] = pieces[s][:TXT, i * HD : (i + 1) * HD]
        rows = att[s // 2][...] if s % 2 == 0 else pieces[s][:, 3 * HD :]
        att_ref[:, at] = dot_nn(order_ref[...], rows).astype(BF)


def unfold(meta, pieces, att):
    return pl.pallas_call(
        unfold_kernel,
        out_shape=[jax.ShapeDtypeStruct((3, TXT, 4 * HD), BF), jax.ShapeDtypeStruct((TOK, 4 * HD), BF)],
        in_specs=[smem()] + [vmem()] * 6,
        out_specs=[vmem()] * 2,
        scratch_shapes=[pltpu.VMEM((TOK, TOK), BF)],
        compiler_params=pltpu.CompilerParams(vmem_limit_bytes=8 * MIB),
        cost_estimate=pl.CostEstimate(flops=8 * TOK * TOK * HD, bytes_accessed=4 * MIB, transcendentals=0),
        name="unfold",
    )(meta, *pieces, *att)


def slope_kernel(above_ref, eg_ref, below_ref, features_ref, conv_ref, out_ref, wide_ref):
    wide_ref[0, :10] = above_ref[...].astype(F32)
    for i in range(4):
        wide_ref[i + 1, :10] = eg_ref[...].astype(F32)[10 * i : 10 * i + 10]
    wide_ref[5, :10] = below_ref[...].astype(F32)
    value = features_ref[...].astype(F32)
    sigma = 1.0 / (1.0 + jnp.exp(-value))
    slope = sigma * (1.0 + value * (1.0 - sigma))
    total = jnp.zeros(out_ref.shape, F32)
    for a in range(3):
        for b in range(3):
            window = wide_ref[2 - a : 6 - a, 2 - b : 10 - b, :].reshape(out_ref.shape).astype(BF)
            total = total + dot_nt(window, conv_ref[a, b])
    center = wide_ref[1:5, 1:9, :].reshape(out_ref.shape)
    out_ref[...] = (center + slope * total).astype(BF)


def slope(above, eg, below, features, conv_weight):
    channels = features.shape[1]
    return pl.pallas_call(
        slope_kernel,
        out_shape=jax.ShapeDtypeStruct(features.shape, BF),
        in_specs=[vmem()] * 5,
        out_specs=vmem(),
        scratch_shapes=[pltpu.VMEM((6, 16, channels), F32)],
        compiler_params=pltpu.CompilerParams(vmem_limit_bytes=12 * MIB),
        name="slope",
    )(above, eg, below, features, conv_weight)


def local(features, conv_weight, w_query_key, w_value, text_qkv, span_ids, out_cot):
    seq = lax.axis_index("seq")
    y, j = seq // 4, seq % 4
    rows, columns, channels = features.shape
    up = [(i, i + 1) for i in range(15)]
    down = [(i + 1, i) for i in range(15)]
    shift_y = [[(i, (i + 4 * s) % 16) for i in range(16)] for s in range(4)]
    swap_core = [(i, i ^ 1) for i in range(16)]
    swap_x = [(i, i ^ 2) for i in range(16)]

    copies = jnp.broadcast_to(features[None], (8,) + features.shape)
    band = lax.all_to_all(copies, "col", 0, 0, tiled=True)
    above = lax.ppermute(band[:, rows - 1], "seq", up)
    below = lax.ppermute(band[:, 0], "seq", down)

    spans = span_ids.reshape(16, TOK)
    offsets = jnp.arange(TOK, dtype=jnp.int32)
    first = jnp.min(jnp.where(spans >= 0, offsets[None, :], TOK), axis=1)
    span = jnp.max(spans, axis=1)
    ends, starts = spans[3:15:4, -1], spans[4:16:4, 0]
    joined = (ends >= 0) & (ends == starts) & (j == 3)
    scalars = [jnp.stack([y, j]), joined, jnp.zeros((3,), jnp.int32), first, span]
    meta = jnp.concatenate([part.astype(jnp.int32) for part in scalars])

    w_qk = w_query_key.reshape(channels, 8 * HD)
    g = turn(meta, jnp.transpose(out_cot.reshape(TOK, 4, HD), (1, 0, 2)))
    g = [lax.ppermute(g[s], "seq", shift_y[s]) if s else g[0] for s in range(4)]
    acc = inner(band, conv_weight)
    above, below, acc, g = lax.optimization_barrier((above, below, acc, g))
    out = encode(meta, acc, above, below, conv_weight, w_qk, w_value, text_qkv.reshape(TXT, 12 * HD))
    q = list(out[4:])
    own = [out[0], jnp.concatenate([lax.ppermute(out[s], "seq", shift_y[s]) for s in ORDER[:3]])]
    crossed = [lax.ppermute(own[0], "seq", swap_x)]
    q[1], q[2], q[3], own[1], crossed[0] = lax.optimization_barrier((q[1], q[2], q[3], own[1], crossed[0]))
    q = [lax.ppermute(q[s], "seq", shift_y[s]) if s else q[0] for s in range(4)]
    crossed.append(lax.ppermute(own[1], "seq", swap_x))
    near_kv = own + [lax.ppermute(piece, "seq", swap_core) for piece in own]
    q, g, *state = forward((0, 1), meta, q + g, near_kv)
    crossed, state = lax.optimization_barrier((crossed, state))
    far_kv = crossed + [lax.ppermute(piece, "seq", swap_core) for piece in crossed]
    *att, lse, delta = forward((2, 3), meta, [q, g, *state], far_kv)
    stats = [q, g, lse, delta]

    def back(piece, s):
        return lax.ppermute(piece, "seq", shift_y[4 - s])

    dq, keep, send = backward((2, 3), meta, stats, [], far_kv)
    far = (keep.astype(F32) + lax.ppermute(send, "seq", swap_core).astype(F32)).astype(BF)
    far, dq = lax.optimization_barrier((far, dq))
    far = [lax.ppermute(far[a * TOK : (a + 2) * TOK], "seq", swap_x) for a in (0, 2)]
    dq, keep, send = backward((0, 1), meta, stats, dq, near_kv)
    att2 = back(att[2], 2)
    far[0], dq, keep, send, att2 = lax.optimization_barrier((far[0], dq, keep, send, att2))
    recv = lax.ppermute(send, "seq", swap_core)
    piece1, piece3 = merge((0, 1), keep, recv, far[0], [dq[1], dq[3]], [att[1], att[3]])
    piece1, piece3 = back(piece1, 1), back(piece3, 3)
    piece2, piece0 = merge((2, 3), keep, recv, far[1], [dq[2], dq[0]], [])
    piece2 = back(piece2, 2)
    pieces = [piece0, piece3, piece2, piece1]
    parts = project(meta, w_qk, w_value, pieces)
    parts, pieces = lax.optimization_barrier((parts, pieces))
    text_grad, attended = unfold(meta, pieces, [att[0], att2])
    text_grad = jnp.transpose(text_grad, (1, 0, 2))

    conv_weight, parts = lax.optimization_barrier((conv_weight, parts))
    taps = stage(conv_weight)
    parts = lax.all_to_all(parts, "col", 0, 0, tiled=True)
    parts, text_grad, attended = lax.optimization_barrier((parts, text_grad, attended))
    eg = jnp.sum(parts.astype(F32), axis=0).astype(BF)
    eg_above = lax.ppermute(eg[30:], "seq", up)
    eg_below = lax.ppermute(eg[:10], "seq", down)
    feature_grad = slope(eg_above, eg, eg_below, features.reshape(rows * columns, channels), taps)
    return (attended, feature_grad.reshape(features.shape), text_grad)


def solution(mesh):
    in_specs = (
        P("seq", "col", None),
        P(),
        P(None, None, "col"),
        P(None, "col"),
        P("seq", None, "col"),
        P(),
        P("seq", "col"),
    )
    out_specs = (P("seq", "col"), P("seq", "col", None), P("seq", None, "col"))
    return jax.shard_map(local, mesh=mesh, in_specs=in_specs, out_specs=out_specs, check_vma=False)
```
